256 devices in a mesh: step: 8 (over x, core), seq: 32 (over z, y).
Axes of the slice: x: 4, y: 4, z: 8, core: 2. Of those that a mesh axis runs over, the one named last changes fastest.
Arguments:
- step_index: int32 [9], replicated, may hold values from 207 to 999, as said below
- window_init: float32 [8, 1024, 4096], P('step', 'seq'), may hold values from -15 to 15
- qkv_weight: bfloat16 [3, 4096, 4096], P(None, None, 'seq'), may hold values from -2.5 to 2.5
Outputs:
- advanced: float32 [8, 1024, 4096], P('step', 'seq')
- residuals: float32 [2], replicated
The draws below stay inside these ranges and needn't reach their ends.
Inputs may be any that keep to these rules, and one draw needn't show every extreme that they name: `step_index`: strictly falling; the first entry is 999 and neighbours differ by 40 to 99.
All inputs are finite; a program needn't handle non-finite values.
Results may differ from the reference program's by a relative error of at most 0.004.
Values may be sent and summed in bfloat16 or wider, within the bound.
No kernel may reach another device: no remote copies, remote signals or barrier semaphores. Data moves between devices by JAX's collectives and lax.ppermute only.
A program may use at most 64 MiB of HBM per device.

```python
import math
import jax
import jax.numpy as jnp
from jax import lax

T_DEV = 32
HD = 128
ITERS = 2
STEPS = 8
TOKENS = 1024
HEADS = 32
D = 4096


def draw_step_index(key, part):
    key = jax.random.fold_in(key, 11)
    gaps = jax.random.randint(key, (STEPS + 1,), 40, 100)
    return (999 + gaps[0] - jnp.cumsum(gaps)).astype(jnp.int32)


def draw_window_init(key, part):
    key = jax.random.fold_in(key, 23)
    first_key = jax.random.fold_in(key, 0)
    third_key = jax.random.fold_in(key, 2)
    fourth_key = jax.random.fold_in(key, 3)
    profile = 0.5 + jnp.arange(TOKENS, dtype=jnp.float32) / TOKENS
    block_count = TOKENS // T_DEV
    ranking = jax.random.permutation(third_key, block_count)
    warm_block = (ranking < block_count // 2).astype(jnp.float32)
    warm_token = jnp.repeat(warm_block, T_DEV)
    later_step = (jnp.arange(STEPS) >= 1).astype(jnp.float32)
    settled = later_step[:, None, None] * warm_token[None, :, None]
    values = jax.random.truncated_normal(first_key, -5.0, 5.0, (STEPS, TOKENS, D), jnp.float32) * profile[None, :, None]
    jitter = 0.05 * jax.random.truncated_normal(fourth_key, -5.0, 5.0, (STEPS, TOKENS, D), jnp.float32)
    near_start = values[0:1] + jitter * profile[None, :, None]
    values = values * (1.0 - settled) + near_start * settled
    return values.astype(jnp.float32)


def draw_qkv_weight(key, part):
    key = jax.random.fold_in(key, 37)
    key_one = jax.random.fold_in(key, 0)
    key_two = jax.random.fold_in(key, 1)
    key_four = jax.random.fold_in(key, 3)
    spread = 1.0 / jnp.sqrt(jnp.float32(D))
    keys_part = 1.6 * spread * jax.random.truncated_normal(key_one, -5.0, 5.0, (D, D), jnp.float32)
    values_part = 1.5 * spread * jax.random.truncated_normal(key_two, -5.0, 5.0, (D, D), jnp.float32)
    fresh = 1.6 * spread * jax.random.truncated_normal(key_four, -5.0, 5.0, (D, D), jnp.float32)
    queries = fresh
    stacked = jnp.stack([queries, keys_part, values_part])
    return jnp.clip(stacked, -2.5, 2.5).astype(jnp.bfloat16)


def setup_inputs(seed: int = 0) -> dict:
    arg_keys = jax.random.split(jax.random.key(seed), 4)
    return {
        "step_index": draw_step_index(jax.random.fold_in(arg_keys[3], 71), 0),
        "window_init": draw_window_init(jax.random.fold_in(arg_keys[3], 71), 0),
        "qkv_weight": draw_qkv_weight(jax.random.fold_in(arg_keys[3], 71), 0),
    }


def layer_norm(values):
    center = lax.optimization_barrier(jnp.mean(values, axis=-1, keepdims=True))
    spread = lax.optimization_barrier(jnp.mean((values - center) ** 2, axis=-1, keepdims=True))
    return (values - center) * lax.rsqrt(spread + 1e-05)

def attend(query, keys, values):
    total_rows = query.shape[0]
    width_head = query.shape[1]
    block_size = min(512, total_rows)
    score_scale = 1.0 / math.sqrt(width_head)

    def one_block(rows):
        scores = jnp.dot(rows, keys.T, preferred_element_type=jnp.float32) * score_scale
        row_peak = lax.optimization_barrier(jnp.max(scores, axis=-1, keepdims=True))
        expo = jnp.exp(scores - row_peak)
        weights = (expo / lax.optimization_barrier(jnp.sum(expo, axis=-1, keepdims=True))).astype(jnp.bfloat16)
        return jnp.dot(weights, values, preferred_element_type=jnp.float32).astype(jnp.bfloat16)
    blocks = query.reshape(total_rows // block_size, block_size, width_head)
    return lax.map(one_block, blocks).reshape(total_rows, width_head)

def drift_input(current_step, qkv_weight):
    normed = layer_norm(current_step).astype(jnp.bfloat16)
    query = jnp.dot(normed, qkv_weight[0], preferred_element_type=jnp.float32).astype(jnp.bfloat16)
    keys = jnp.dot(normed, qkv_weight[1], preferred_element_type=jnp.float32).astype(jnp.bfloat16)
    values = jnp.dot(normed, qkv_weight[2], preferred_element_type=jnp.float32).astype(jnp.bfloat16)
    query = query.reshape(TOKENS, HEADS, HD).transpose(1, 0, 2)
    keys = keys.reshape(TOKENS, HEADS, HD).transpose(1, 0, 2)
    values = values.reshape(TOKENS, HEADS, HD).transpose(1, 0, 2)
    heads_out = lax.map(lambda trio: attend(trio[0], trio[1], trio[2]), (query, keys, values))
    attended = heads_out.transpose(1, 0, 2).reshape(TOKENS, D)
    return attended.astype(jnp.float32) - current_step

def reference(step_index, window_init, qkv_weight):
    step_width = (step_index[:-1] - step_index[1:]).astype(jnp.float32) / 1000.0
    anchor = window_init[0]
    current = window_init
    gap_list = []
    advanced = current
    for sweep in range(ITERS):
        drifts = lax.map(lambda one_step: drift_input(one_step, qkv_weight), current)
        increment = step_width[:, None, None] * drifts
        earlier = jnp.cumsum(increment[:-1], axis=0)
        before = jnp.concatenate([jnp.zeros_like(increment[:1]), earlier], axis=0)
        updated = anchor[None] + before
        squared = jnp.sum((updated - current) ** 2)
        gap_list.append(jnp.sqrt(squared / (STEPS * TOKENS * D)))
        advanced = updated + increment
        current = updated
    return (advanced, jnp.stack(gap_list))
```

```python
import math

import jax
import jax.numpy as jnp
from jax import lax
from jax.experimental import pallas as pl
from jax.experimental.pallas import tpu as pltpu
from jax.sharding import Mesh, PartitionSpec as P

HD = 128
ITERS = 2
SIZES = {"x": 4, "c": 2, "z": 8, "y": 4}
STEP = ("x", "c")
SEQ = ("z", "y")
ALL = STEP + SEQ
HALF = 16


def shift(x, axis, by):
    n = SIZES[axis]
    return lax.ppermute(x, axis, [(i, (i + by) % n) for i in range(n)])


def ring(x, axis):
    n = SIZES[axis]
    middle = n // 2
    out = [None] * n
    out[0] = x
    up = down = x
    for d in range(1, middle):
        up, down = shift(up, axis, 1), shift(down, axis, -1)
        out[n - d], out[d] = up, down
    rows = x.shape[0] // 2
    out[middle] = jnp.concatenate([shift(up[:rows], axis, 1), shift(down[rows:], axis, -1)])
    return out


def gather_tokens(x):
    first, second = x[:HALF], x[HALF:]
    along_y = jnp.concatenate(ring(first, "y"))
    along_z = jnp.concatenate(ring(second, "z"))
    return ring(along_y, "z") + ring(along_z, "y")


def layer_norm(values):
    center = jnp.mean(values, axis=-1, keepdims=True)
    spread = jnp.mean((values - center) ** 2, axis=-1, keepdims=True)
    return (values - center) * lax.rsqrt(spread + 1e-05)


def attend_kernel(place, qkv_ref, out_ref):
    factor = math.log2(math.e) / math.sqrt(HD)
    z, y = place[0], place[1]
    keys = qkv_ref[:, HD : 2 * HD]
    values = qkv_ref[:, 2 * HD :]
    block = 256
    for b in range(qkv_ref.shape[0] // block):
        query = qkv_ref[b * block : (b + 1) * block, :HD]
        scores = lax.dot_general(
            query, keys, (((1,), (1,)), ((), ())), preferred_element_type=jnp.float32
        )
        peak = jnp.max(scores, axis=-1, keepdims=True)
        expo = jnp.exp2((scores - peak) * factor)
        total = jnp.sum(expo, axis=-1, keepdims=True)
        mixed = jnp.dot(expo.astype(jnp.bfloat16), values, preferred_element_type=jnp.float32)
        mixed = (mixed / total).astype(jnp.bfloat16)
        for r in range(block // HALF):
            g = b * (block // HALF) + r
            if g < 32:
                dz, dy, half = g // 4, g % 4, 0
            else:
                dz, dy, half = (g - 32) % 8, (g - 32) // 8, 1
            s = lax.rem(z + dz, 8) * 4 + lax.rem(y + dy, 4)
            out_ref[s, half * HALF : (half + 1) * HALF, :] = mixed[r * HALF : (r + 1) * HALF]


def attend(place, qkv):
    return pl.pallas_call(
        attend_kernel,
        out_shape=jax.ShapeDtypeStruct((32, 32, HD), jnp.bfloat16),
        in_specs=[
            pl.BlockSpec(memory_space=pltpu.SMEM),
            pl.BlockSpec(memory_space=pltpu.VMEM),
        ],
        out_specs=pl.BlockSpec(memory_space=pltpu.VMEM),
        compiler_params=pltpu.CompilerParams(vmem_limit_bytes=32 * 1024 * 1024),
        cost_estimate=pl.CostEstimate(
            flops=4 * 1024 * 1024 * HD, bytes_accessed=2**20, transcendentals=2**20
        ),
    )(place, qkv)


def exchange_all(pieces):
    return lax.all_to_all(pieces, ALL, split_axis=0, concat_axis=0, tiled=True)


def to_heads(rows):
    return rows.reshape(8, 4, 32, HD).transpose(0, 2, 1, 3)


def to_tokens(pieces):
    return pieces.reshape(8, 32, 4, HD).transpose(0, 2, 1, 3).reshape(32, 32 * HD)


def split3(value):
    high = value.astype(jnp.bfloat16)
    rest = value - high.astype(jnp.float32)
    mid = rest.astype(jnp.bfloat16)
    low = (rest - mid.astype(jnp.float32)).astype(jnp.bfloat16)
    return high, mid, low


def local(step_index, window_init, qkv_weight):
    window = window_init[0]
    step_rank = lax.axis_index(STEP)
    place = jnp.stack([lax.axis_index("z"), lax.axis_index("y")]).astype(jnp.int32)
    widths = (step_index[:-1] - step_index[1:]).astype(jnp.float32) / 1000.0
    weight = qkv_weight.transpose(1, 0, 2).reshape(-1, 3 * HD)
    anchor = lax.psum(jnp.where(step_rank == 0, window, jnp.zeros_like(window)), STEP)
    current = exchange_all(to_heads(window).reshape(256, 4, HD)).reshape(8, 32, 4, HD)
    start = current[0]

    def drift(rows):
        normed = layer_norm(rows).astype(jnp.bfloat16)
        projected = [
            jnp.dot(block, weight, preferred_element_type=jnp.float32).astype(jnp.bfloat16)
            for block in gather_tokens(normed)
        ]
        attended = attend(place, jnp.concatenate(projected))
        pieces = attended.reshape(32, 8, 4, HD).transpose(1, 0, 2, 3)
        return lax.all_to_all(pieces, STEP, split_axis=0, concat_axis=0, tiled=True)

    rows = window
    gaps = []
    for sweep in range(ITERS):
        attended = drift(rows).astype(jnp.float32)
        before = [jnp.zeros_like(start)]
        for k in range(8):
            before.append(before[k] + widths[k] * (attended[k] - current[k]))
        updated = start[None] + jnp.stack(before[:8])
        gaps.append(jnp.sum((updated - current) ** 2))
        current = updated
        if sweep < ITERS - 1:
            sent = jnp.stack(before[:8]).astype(jnp.bfloat16).reshape(256, 4, HD)
            rows = anchor + to_tokens(exchange_all(sent)).astype(jnp.float32)
    sent = jnp.stack(before[1:]).astype(jnp.bfloat16).reshape(256, 4, HD)
    marks = jnp.stack(split3(gaps[0]) + split3(gaps[1]) + (jnp.bfloat16(0),) * 2)
    extra = jnp.broadcast_to(
        jnp.concatenate([marks, jnp.zeros((HD - 8,), jnp.bfloat16)])[None, None],
        (256, 4, HD),
    )
    got = exchange_all(jnp.concatenate([sent, extra], axis=1))
    advanced = anchor + to_tokens(got[:, :4]).astype(jnp.float32)
    parts = got[:, 4, :6].astype(jnp.float32).reshape(256, 2, 3)
    totals = jnp.sum(parts, axis=(0, 2))
    residuals = jnp.sqrt(totals / (8 * 1024 * 4096))
    return (advanced[None], residuals)


def solution(mesh):
    fine = Mesh(mesh.devices.reshape(4, 2, 8, 4), ALL)
    placed = (P(), P(STEP, SEQ, None), P(None, None, SEQ))
    return jax.shard_map(
        local, mesh=fine, in_specs=placed, out_specs=(P(STEP, SEQ, None), P()), check_vma=False
    )
```

```python
import math

import jax
import jax.numpy as jnp
from jax import lax
from jax.experimental import pallas as pl
from jax.experimental.pallas import tpu as pltpu
from jax.sharding import Mesh, PartitionSpec as P

HD = 128
HEADS = 32
D = HEADS * HD
STEPS = 8
TOKENS = 1024
SIZES = {"x": 4, "c": 2, "z": 8, "y": 4}
STEP = ("x", "c")
SEQ = ("z", "y")
ALL = STEP + SEQ
HALF = 16
MIB = 1024 * 1024


def shift(x, axis, by):
    n = SIZES[axis]
    return lax.ppermute(x, axis, [(i, (i + by) % n) for i in range(n)])


def ring(x, axis):
    n = SIZES[axis]
    middle = n // 2
    out = [None] * n
    out[0] = x
    up = down = x
    for d in range(1, middle):
        up, down = shift(up, axis, 1), shift(down, axis, -1)
        out[n - d], out[d] = up, down
    rows = x.shape[0] // 2
    out[middle] = jnp.concatenate([shift(up[:rows], axis, 1), shift(down[rows:], axis, -1)])
    return out


SMALL_Y = (0, 3, 1, 2)
SMALL_Z = (0, 4, 7, 3, 1, 5, 2, 6)


def small_y(x):
    return jnp.concatenate([x, shift(x, "y", 1), shift(x, "y", -1), shift(x, "y", 2)])


def small_z(x):
    pair = jnp.concatenate([x, shift(x, "z", 4)])
    return jnp.concatenate(
        [pair, shift(pair, "z", 1), shift(pair, "z", -1), shift(pair, "z", -2)]
    )


EARLY_Z, LATE_Z = (0, 1, 7, 2, 6), (3, 5, 4)
EARLY_Y, LATE_Y = (0,), (1, 3, 2)


def gather_tokens(x):
    by_z = ring(small_y(x[:HALF]), "z")
    by_y = ring(small_z(x[HALF:]), "y")
    early = [by_z[d] for d in EARLY_Z] + [by_y[d] for d in EARLY_Y]
    late = [by_z[d] for d in LATE_Z] + [by_y[d] for d in LATE_Y]
    return early, late


def row_blocks():
    places = []
    for far_z, far_y in ((EARLY_Z, EARLY_Y), (LATE_Z, LATE_Y)):
        places += [(dz, dy, 0) for dz in far_z for dy in SMALL_Y]
        places += [(dz, dy, 1) for dy in far_y for dz in SMALL_Z]
    return places


def project_rows(blocks, weight_ref, rows_ref):
    start = 0
    for block in blocks:
        rows_ref[start : start + block.shape[0], :] = block[...]
        start += block.shape[0]
    out = jnp.dot(rows_ref[...], weight_ref[...], preferred_element_type=jnp.float32)
    return out.astype(jnp.bfloat16)


def project_kernel(*refs):
    *blocks, weight_ref, out_ref, rows_ref = refs
    out_ref[...] = project_rows(blocks, weight_ref, rows_ref)


def project(blocks, weight):
    rows = sum(b.shape[0] for b in blocks)
    return pl.pallas_call(
        project_kernel,
        out_shape=jax.ShapeDtypeStruct((rows, 3 * HD), jnp.bfloat16),
        in_specs=[pl.BlockSpec(memory_space=pltpu.VMEM)] * (len(blocks) + 1),
        out_specs=pl.BlockSpec(memory_space=pltpu.VMEM),
        scratch_shapes=[pltpu.VMEM((rows, D), jnp.bfloat16)],
        compiler_params=pltpu.CompilerParams(vmem_limit_bytes=24 * MIB),
        cost_estimate=pl.CostEstimate(
            flops=6 * rows * D * HD, bytes_accessed=2 * rows * D, transcendentals=0
        ),
    )(*blocks, weight)


def attend_kernel(place, early_ref, *refs):
    *blocks, weight_ref, out_ref, rows_ref, qkv_ref = refs
    early = early_ref.shape[0]
    qkv_ref[:early, :] = early_ref[...]
    qkv_ref[early:, :] = project_rows(blocks, weight_ref, rows_ref)
    factor = math.log2(math.e) / math.sqrt(HD)
    z, y = place[0], place[1]
    keys = qkv_ref[:, HD : 2 * HD]
    values = qkv_ref[:, 2 * HD :]
    places = row_blocks()
    size = 256
    for b in range(TOKENS // size):
        query = qkv_ref[b * size : (b + 1) * size, :HD]
        scores = lax.dot_general(
            query, keys, (((1,), (1,)), ((), ())), preferred_element_type=jnp.float32
        )
        peak = jnp.max(scores, axis=-1, keepdims=True)
        expo = jnp.exp2((scores - peak) * factor)
        total = jnp.sum(expo, axis=-1, keepdims=True)
        mixed = jnp.dot(expo.astype(jnp.bfloat16), values, preferred_element_type=jnp.float32)
        mixed = (mixed / total).astype(jnp.bfloat16)
        for r in range(size // HALF):
            dz, dy, half = places[b * (size // HALF) + r]
            s = lax.rem(z + dz, 8) * 4 + lax.rem(y + dy, 4)
            out_ref[s, half * HALF : (half + 1) * HALF, :] = mixed[r * HALF : (r + 1) * HALF]


def attend(place, early, blocks, weight):
    rows = sum(b.shape[0] for b in blocks)
    vmem = pl.BlockSpec(memory_space=pltpu.VMEM)
    return pl.pallas_call(
        attend_kernel,
        out_shape=jax.ShapeDtypeStruct((TOKENS // 32, 32, HD), jnp.bfloat16),
        in_specs=[pl.BlockSpec(memory_space=pltpu.SMEM)] + [vmem] * (len(blocks) + 2),
        out_specs=vmem,
        scratch_shapes=[
            pltpu.VMEM((rows, D), jnp.bfloat16),
            pltpu.VMEM((TOKENS, 3 * HD), jnp.bfloat16),
        ],
        compiler_params=pltpu.CompilerParams(vmem_limit_bytes=32 * MIB),
        cost_estimate=pl.CostEstimate(
            flops=4 * TOKENS * TOKENS * HD + 6 * rows * D * HD,
            bytes_accessed=2 * rows * D,
            transcendentals=TOKENS * TOKENS,
        ),
    )(place, early, *blocks, weight)


def norm(values):
    center = jnp.mean(values, axis=-1, keepdims=True)
    moved = values - center
    spread = jnp.mean(moved * moved, axis=-1, keepdims=True)
    return moved * lax.rsqrt(spread + 1e-05)


def norm_kernel(rows_ref, out_ref):
    out_ref[...] = norm(rows_ref[...]).astype(jnp.bfloat16)


def layer_norm(rows):
    return pl.pallas_call(
        norm_kernel, out_shape=jax.ShapeDtypeStruct(rows.shape, jnp.bfloat16)
    )(rows)


def sweep_kernel(width, attended_ref, anchor_ref, current_ref, out_ref, gap_ref, *updated_ref):
    anchor = anchor_ref[0]
    before = jnp.zeros_like(anchor)
    gap = jnp.zeros_like(anchor)
    for k in range(STEPS):
        current = current_ref[k]
        increment = width[k] * (attended_ref[k].astype(jnp.float32) - current)
        updated = anchor + before
        change = updated - current
        gap = gap + change * change
        if updated_ref:
            updated_ref[0][k] = updated
            out_ref[k] = norm(updated).astype(jnp.bfloat16)
        else:
            out_ref[k] = updated + increment
        before = before + increment
    gap_ref[...] = jnp.broadcast_to(jnp.sum(gap), gap_ref.shape)


def sweep_update(width, attended, anchor, current, last):
    shape = current.shape
    vmem = pl.BlockSpec(memory_space=pltpu.VMEM)
    outs = [
        jax.ShapeDtypeStruct(shape, jnp.float32 if last else jnp.bfloat16),
        jax.ShapeDtypeStruct((1, 128), jnp.float32),
    ]
    if not last:
        outs.append(jax.ShapeDtypeStruct(shape, jnp.float32))
    return pl.pallas_call(
        sweep_kernel,
        out_shape=outs,
        in_specs=[pl.BlockSpec(memory_space=pltpu.SMEM)] + [vmem] * 3,
        out_specs=[vmem] * len(outs),
    )(width, attended, anchor, current)


def over_step(pieces):
    return lax.all_to_all(pieces, STEP, split_axis=0, concat_axis=0, tiled=True)


def over_all(pieces):
    return lax.all_to_all(pieces, ALL, split_axis=0, concat_axis=0, tiled=True)


def local(step_index, window_init, qkv_weight):
    window = window_init[0]
    place = jnp.stack([lax.axis_index("z"), lax.axis_index("y")]).astype(jnp.int32)
    width = (step_index[:-1] - step_index[1:]).astype(jnp.float32) / 1000.0
    weight = qkv_weight.transpose(1, 0, 2).reshape(D, 3 * HD)
    start = over_step(window.reshape(STEPS, 4, D))

    def drift(normed):
        early, late = gather_tokens(normed)
        attended = attend(place, project(early, weight), late, weight)
        pieces = attended.reshape(32, STEPS, 4, HD).transpose(1, 0, 2, 3)
        got = over_all(pieces.reshape(256, 4, HD)).reshape(STEPS, HEADS, 4, HD)
        return got.transpose(0, 2, 1, 3).reshape(STEPS, 4, D)

    attended = drift(layer_norm(window))
    normed, first_gap, updated = sweep_update(width, attended, start[:1], start, False)
    attended = drift(over_step(normed).reshape(32, D))
    advanced, second_gap = sweep_update(width, attended, start[:1], updated, True)
    marks = jnp.concatenate([first_gap, second_gap])[None]
    totals = jnp.sum(over_all(jnp.broadcast_to(marks, (256, 2, 128))), axis=0)[:, 0]
    residuals = jnp.sqrt(totals / (STEPS * TOKENS * D))
    return (over_step(advanced).reshape(1, 32, D), residuals)


def solution(mesh):
    fine = Mesh(mesh.devices.reshape(4, 2, 8, 4), ALL)
    placed = (P(), P(STEP, SEQ, None), P(None, None, SEQ))
    return jax.shard_map(
        local, mesh=fine, in_specs=placed, out_specs=(P(STEP, SEQ, None), P()), check_vma=False
    )
```

```python
import functools
import math

import jax
import jax.numpy as jnp
from jax import lax
from jax.experimental import pallas as pl
from jax.experimental.pallas import tpu as pltpu
from jax.sharding import Mesh, PartitionSpec as P

HD = 128
HEADS = 32
D = HEADS * HD
STEPS = 8
TOKENS = 1024
SIZES = {"x": 4, "c": 2, "z": 8, "y": 4}
STEP = ("x", "c")
SEQ = ("z", "y")
ALL = STEP + SEQ
HALF = 16
MIB = 1024 * 1024


def shift(x, axis, by):
    n = SIZES[axis]
    pairs = []
    for i in range(n):
        if axis == "x":
            pairs += [(2 * i, 2 * ((i + by) % n)), (2 * i + 1, 2 * ((i - by) % n) + 1)]
        else:
            pairs += [(i, (i + by) % n), (n + i, n + (i - by) % n)]
    return lax.ppermute(x, ("x", "c") if axis == "x" else ("c", axis), pairs)


def swap(x):
    return lax.ppermute(x, "c", [(0, 1), (1, 0)])


def join_kernel(*refs):
    *blocks, out_ref = refs
    start = 0
    for block in blocks:
        out_ref[start : start + block.shape[0], :] = block[...]
        start += block.shape[0]


def join(blocks):
    rows = sum(b.shape[0] for b in blocks)
    return pl.pallas_call(
        join_kernel,
        out_shape=jax.ShapeDtypeStruct((rows, D), jnp.bfloat16),
        in_specs=[pl.BlockSpec(memory_space=pltpu.VMEM)] * len(blocks),
        out_specs=pl.BlockSpec(memory_space=pltpu.VMEM),
        compiler_params=pltpu.CompilerParams(vmem_limit_bytes=8 * MIB),
        cost_estimate=pl.CostEstimate(flops=0, bytes_accessed=4 * rows * D, transcendentals=0),
    )(*blocks)


def ring(x, axis):
    n = SIZES[axis]
    out = {0: x}
    up = down = x
    for d in range(1, n // 2):
        up, down = shift(up, axis, 1), shift(down, axis, -1)
        out[-d], out[d] = up, down
    out[-(n // 2)] = shift(up, axis, 1)
    return out


SMALL_4 = (0, -1, 1, -2)
SMALL_Z = (0, -4, -1, -5, 1, -3, 2, -2)


def small_4(x, axis):
    return join([x, shift(x, axis, 1), shift(x, axis, -1), shift(x, axis, 2)])


def small_z(x):
    pair = join([x, shift(x, "z", 4)])
    return join([pair, shift(pair, "z", 1), shift(pair, "z", -1), shift(pair, "z", -2)])


EARLY_Z, LATE_Z = (0, -1, 1, -2, 2), (-3, 3, -4)
EARLY_4, LATE_4 = (0, -1, 1), (-2,)


def gather_long(x):
    by_z = ring(small_4(x[:HALF], "y"), "z")
    by_y = ring(small_z(x[HALF:]), "y")
    early = [by_z[d] for d in EARLY_Z] + [by_y[0]]
    late = [by_z[d] for d in LATE_Z] + [by_y[d] for d in (-1, 1, -2)]
    return early, late


def places_long():
    places = []
    for far_z, far_y in ((EARLY_Z, (0,)), (LATE_Z, (-1, 1, -2))):
        places += [(dz, dy, 0, 0) for dz in far_z for dy in SMALL_4]
        places += [(dz, dy, 1, 0) for dy in far_y for dz in SMALL_Z]
    return places


def gather_short(x):
    by_x = ring(small_4(x[:HALF], "y"), "x")
    by_y = ring(small_4(x[HALF:], "x"), "y")
    early = [by_x[d] for d in EARLY_4] + [by_y[d] for d in EARLY_4]
    late = [by_x[d] for d in LATE_4] + [by_y[d] for d in LATE_4]
    return early + [swap(b) for b in early], late + [swap(b) for b in late]


def places_short():
    places = []
    for far in (EARLY_4, LATE_4):
        for core in (0, 1):
            places += [(dx, dy, 0, core) for dx in far for dy in SMALL_4]
            places += [(dx, dy, 1, core) for dy in far for dx in SMALL_4]
    return places


def project_rows(blocks, weight_ref, rows_ref):
    start = 0
    for block in blocks:
        rows_ref[start : start + block.shape[0], :] = block[...]
        start += block.shape[0]
    out = jnp.dot(rows_ref[...], weight_ref[...], preferred_element_type=jnp.float32)
    return out.astype(jnp.bfloat16)


def project_kernel(*refs):
    *blocks, weight_ref, out_ref, rows_ref = refs
    out_ref[...] = project_rows(blocks, weight_ref, rows_ref)


def project(blocks, weight):
    rows = sum(b.shape[0] for b in blocks)
    return pl.pallas_call(
        project_kernel,
        out_shape=jax.ShapeDtypeStruct((rows, 3 * HD), jnp.bfloat16),
        in_specs=[pl.BlockSpec(memory_space=pltpu.VMEM)] * (len(blocks) + 1),
        out_specs=pl.BlockSpec(memory_space=pltpu.VMEM),
        scratch_shapes=[pltpu.VMEM((rows, D), jnp.bfloat16)],
        compiler_params=pltpu.CompilerParams(vmem_limit_bytes=24 * MIB),
        cost_estimate=pl.CostEstimate(
            flops=6 * rows * D * HD, bytes_accessed=2 * rows * D, transcendentals=0
        ),
    )(*blocks, weight)


def attend_kernel(short, place, early_ref, *refs):
    *blocks, weight_ref, out_ref, rows_ref, qkv_ref = refs
    early = early_ref.shape[0]
    qkv_ref[:early, :] = early_ref[...]
    qkv_ref[early:, :] = project_rows(blocks, weight_ref, rows_ref)
    factor = math.log2(math.e) / math.sqrt(HD)
    x, core, z, y = place[0], place[1], place[2], place[3]
    keys = qkv_ref[:, HD : 2 * HD]
    values = qkv_ref[:, 2 * HD :]
    places = places_short() if short else places_long()
    size = 256
    for b in range(TOKENS // size):
        query = qkv_ref[b * size : (b + 1) * size, :HD]
        scores = lax.dot_general(
            query, keys, (((1,), (1,)), ((), ())), preferred_element_type=jnp.float32
        )
        peak = jnp.max(scores, axis=-1, keepdims=True)
        expo = jnp.exp2((scores - peak) * factor)
        total = jnp.sum(expo, axis=-1, keepdims=True)
        mixed = jnp.dot(expo.astype(jnp.bfloat16), values, preferred_element_type=jnp.float32)
        mixed = (mixed / total).astype(jnp.bfloat16)
        for r in range(size // HALF):
            far, dy, half, other = places[b * (size // HALF) + r]
            owner = 1 - core if other else core
            sign = 1 - 2 * owner
            row = lax.rem(y + sign * dy + 4, 4)
            if short:
                slot = (2 * lax.rem(x + sign * far + 4, 4) + owner) * 4 + row
            else:
                slot = lax.rem(z + sign * far + 8, 8) * 4 + row
            out_ref[slot, half * HALF : (half + 1) * HALF, :] = mixed[r * HALF : (r + 1) * HALF]


def attend(place, early, blocks, weight, short):
    rows = sum(b.shape[0] for b in blocks)
    vmem = pl.BlockSpec(memory_space=pltpu.VMEM)
    return pl.pallas_call(
        functools.partial(attend_kernel, short),
        out_shape=jax.ShapeDtypeStruct((TOKENS // 32, 32, HD), jnp.bfloat16),
        in_specs=[pl.BlockSpec(memory_space=pltpu.SMEM)] + [vmem] * (len(blocks) + 2),
        out_specs=vmem,
        scratch_shapes=[
            pltpu.VMEM((rows, D), jnp.bfloat16),
            pltpu.VMEM((TOKENS, 3 * HD), jnp.bfloat16),
        ],
        compiler_params=pltpu.CompilerParams(vmem_limit_bytes=32 * MIB),
        cost_estimate=pl.CostEstimate(
            flops=4 * TOKENS * TOKENS * HD + 6 * rows * D * HD,
            bytes_accessed=2 * rows * D,
            transcendentals=TOKENS * TOKENS,
        ),
    )(place, early, *blocks, weight)


def weight_kernel(weight_ref, out_ref):
    for c in range(3):
        out_ref[:, c * HD : (c + 1) * HD] = weight_ref[c]


def side_by_side(weight):
    return pl.pallas_call(
        weight_kernel,
        out_shape=jax.ShapeDtypeStruct((D, 3 * HD), jnp.bfloat16),
        compiler_params=pltpu.CompilerParams(vmem_limit_bytes=16 * MIB),
        cost_estimate=pl.CostEstimate(flops=0, bytes_accessed=12 * D * HD, transcendentals=0),
    )(weight)


def norm(values):
    center = jnp.mean(values, axis=-1, keepdims=True)
    moved = values - center
    spread = jnp.mean(moved * moved, axis=-1, keepdims=True)
    return moved * lax.rsqrt(spread + 1e-05)


def norm_kernel(rows_ref, out_ref):
    out_ref[...] = norm(rows_ref[...]).astype(jnp.bfloat16)


def layer_norm(rows):
    return pl.pallas_call(
        norm_kernel, out_shape=jax.ShapeDtypeStruct(rows.shape, jnp.bfloat16)
    )(rows)


def sweep_kernel(width, attended_ref, anchor_ref, current_ref, out_ref, gap_ref, *updated_ref):
    anchor = anchor_ref[0]
    before = jnp.zeros_like(anchor)
    gap = jnp.zeros_like(anchor)
    for k in range(STEPS):
        current = current_ref[k]
        increment = width[k] * (attended_ref[k].astype(jnp.float32) - current)
        updated = anchor + before
        change = updated - current
        gap = gap + change * change
        if updated_ref:
            updated_ref[0][k] = updated
            out_ref[k] = norm(updated).astype(jnp.bfloat16)
        else:
            out_ref[k] = updated + increment
        before = before + increment
    gap_ref[...] = jnp.broadcast_to(jnp.sum(gap), gap_ref.shape)


def sweep_update(width, attended, anchor, current, last):
    shape = current.shape
    vmem = pl.BlockSpec(memory_space=pltpu.VMEM)
    outs = [
        jax.ShapeDtypeStruct(shape, jnp.float32 if last else jnp.bfloat16),
        jax.ShapeDtypeStruct((1, 128), jnp.float32),
    ]
    if not last:
        outs.append(jax.ShapeDtypeStruct(shape, jnp.float32))
    return pl.pallas_call(
        sweep_kernel,
        out_shape=outs,
        in_specs=[pl.BlockSpec(memory_space=pltpu.SMEM)] + [vmem] * 3,
        out_specs=[vmem] * len(outs),
    )(width, attended, anchor, current)


def over_step(pieces):
    return lax.all_to_all(pieces, STEP, split_axis=0, concat_axis=0, tiled=True)


def over_all(pieces):
    return lax.all_to_all(pieces, ALL, split_axis=0, concat_axis=0, tiled=True)


def local(step_index, window_init, qkv_weight):
    window = window_init[0]
    place = jnp.stack([lax.axis_index(a) for a in ALL]).astype(jnp.int32)
    width = (step_index[:-1] - step_index[1:]).astype(jnp.float32) / 1000.0
    weight = side_by_side(qkv_weight)
    wanted = lax.axis_index(STEP) == lax.axis_index("z")
    other_weight = lax.psum(jnp.where(wanted, weight, jnp.zeros_like(weight)), "z")
    start = over_step(window.reshape(STEPS, 4, D))

    early, late = gather_long(layer_norm(window))
    attended = attend(place, project(early, weight), late, weight, False)
    pieces = attended.reshape(32, STEPS, 4, HD).transpose(1, 0, 2, 3)
    got = over_all(pieces.reshape(256, 4, HD)).reshape(STEPS, HEADS, 4, HD)
    attended = got.transpose(0, 2, 1, 3).reshape(STEPS, 4, D)
    normed, first_gap, updated = sweep_update(width, attended, start[:1], start, False)

    rows = lax.all_to_all(normed, "z", split_axis=0, concat_axis=0, tiled=True).reshape(32, D)
    early, late = gather_short(rows)
    attended = attend(place, project(early, other_weight), late, other_weight, True)
    pieces = attended.reshape(STEPS, 4, 8, 4, HD).transpose(0, 2, 1, 3, 4)
    got = over_all(pieces.reshape(256, 4, HD)).reshape(8, STEPS, 4, 4, HD)
    attended = got.transpose(1, 3, 0, 2, 4).reshape(STEPS, 4, D)
    advanced, second_gap = sweep_update(width, attended, start[:1], updated, True)
    marks = jnp.concatenate([first_gap, second_gap])[None]
    totals = jnp.sum(over_all(jnp.broadcast_to(marks, (256, 2, 128))), axis=0)[:, 0]
    residuals = jnp.sqrt(totals / (STEPS * TOKENS * D))
    return (over_step(advanced).reshape(1, 32, D), residuals)


def solution(mesh):
    fine = Mesh(mesh.devices.reshape(4, 2, 8, 4), ALL)
    placed = (P(), P(STEP, SEQ, None), P(None, None, SEQ))
    return jax.shard_map(
        local, mesh=fine, in_specs=placed, out_specs=(P(STEP, SEQ, None), P()), check_vma=False
    )
```

```python
import functools
import math

import jax
import jax.numpy as jnp
from jax import lax
from jax.experimental import pallas as pl
from jax.experimental.pallas import tpu as pltpu
from jax.sharding import Mesh, PartitionSpec as P

HD = 128
HEADS = 32
D = HEADS * HD
STEPS = 8
TOKENS = 1024
SIZES = {"x": 4, "c": 2, "z": 8, "y": 4}
STEP = ("x", "c")
SEQ = ("z", "y")
ALL = STEP + SEQ
HALF = 16
MIB = 1024 * 1024


def shift(x, axis, by):
    n = SIZES[axis]
    pairs = []
    for i in range(n):
        if axis == "x":
            pairs += [(2 * i, 2 * ((i + by) % n)), (2 * i + 1, 2 * ((i - by) % n) + 1)]
        else:
            pairs += [(i, (i + by) % n), (n + i, n + (i - by) % n)]
    return lax.ppermute(x, ("x", "c") if axis == "x" else ("c", axis), pairs)


def swap(x):
    return lax.ppermute(x, "c", [(0, 1), (1, 0)])


def join_kernel(*refs):
    *blocks, out_ref = refs
    start = 0
    for block in blocks:
        out_ref[start : start + block.shape[0], :] = block[...]
        start += block.shape[0]


def join(blocks):
    rows = sum(b.shape[0] for b in blocks)
    return pl.pallas_call(
        join_kernel,
        out_shape=jax.ShapeDtypeStruct((rows, D), jnp.bfloat16),
        in_specs=[pl.BlockSpec(memory_space=pltpu.VMEM)] * len(blocks),
        out_specs=pl.BlockSpec(memory_space=pltpu.VMEM),
        compiler_params=pltpu.CompilerParams(vmem_limit_bytes=8 * MIB),
        cost_estimate=pl.CostEstimate(flops=0, bytes_accessed=4 * rows * D, transcendentals=0),
    )(*blocks)


SMALL_4 = (0, -1, 1, -2)
SMALL_Z = (0, -4, -1, -5, 1, -3, 2, -2)


def small_4(x, axis):
    return join([x, shift(x, axis, 1), shift(x, axis, -1), shift(x, axis, 2)])


def small_z(x):
    pair = join([x, shift(x, "z", 4)])
    return join([pair, shift(pair, "z", 1), shift(pair, "z", -1), shift(pair, "z", -2)])


def tie(*values):
    return lax.optimization_barrier(values)


def ring_of_4(x, axis):
    up = shift(x, axis, 1)
    return {0: x, -1: up, 1: shift(x, axis, -1), -2: shift(up, axis, 1)}


LONG = (
    ((0, -1, 1), (0,)),
    ((-2, 2, -3, 3), (-1, 1)),
    ((-4,), (-2,)),
)


def gather_long(first, second, window):
    by_z = {0: small_4(first, "y")}
    by_y = ring_of_4(small_z(second), "y")
    by_z[-1], by_z[1] = shift(by_z[0], "z", 1), shift(by_z[0], "z", -1)
    by_z[-2], by_z[2] = shift(by_z[-1], "z", 1), shift(by_z[1], "z", -1)
    _, window = tie(by_z[-1], window)
    window = over_step(window.reshape(STEPS, 4, D))
    by_z[-3], by_z[3] = shift(by_z[-2], "z", 1), shift(by_z[2], "z", -1)
    last, window = tie(by_z[-3], window)
    by_z[-4] = shift(last, "z", 1)
    return [[by_z[d] for d in zs] + [by_y[d] for d in ys] for zs, ys in LONG], window


def places_long():
    places = []
    for far_z, far_y in LONG:
        places += [(dz, dy, 0, 0) for dz in far_z for dy in SMALL_4]
        places += [(dz, dy, 1, 0) for dy in far_y for dz in SMALL_Z]
    return places


SHORT = ((0, -1, 1), (-2,))


def gather_short(x, weight):
    near_y, near_x = small_4(x[:HALF], "y"), small_4(x[HALF:], "x")
    near_y, weight = tie(near_y, weight)
    by_x, by_y = ring_of_4(near_y, "x"), ring_of_4(near_x, "y")
    groups = [[by_x[d] for d in far] + [by_y[d] for d in far] for far in SHORT]
    return [group + [swap(b) for b in group] for group in groups], weight


def places_short():
    places = []
    for far in SHORT:
        for core in (0, 1):
            places += [(dx, dy, 0, core) for dx in far for dy in SMALL_4]
            places += [(dx, dy, 1, core) for dy in far for dx in SMALL_4]
    return places


def project_rows(blocks, weight_ref, rows_ref, sems):
    copies = []
    start = 0
    for n, block in enumerate(blocks):
        rows = block.shape[0]
        copies.append(
            pltpu.make_async_copy(block, rows_ref.at[pl.ds(start, rows), :], sems.at[n])
        )
        copies[-1].start()
        start += rows
    for copy in copies:
        copy.wait()
    out = jnp.dot(rows_ref[...], weight_ref[...], preferred_element_type=jnp.float32)
    return out.astype(jnp.bfloat16)


def project_kernel(*refs):
    *blocks, weight_ref, out_ref, rows_ref, sems = refs
    out_ref[...] = project_rows(blocks, weight_ref, rows_ref, sems)


def project(blocks, weight):
    rows = sum(b.shape[0] for b in blocks)
    vmem = pl.BlockSpec(memory_space=pltpu.VMEM)
    return pl.pallas_call(
        project_kernel,
        out_shape=jax.ShapeDtypeStruct((rows, 3 * HD), jnp.bfloat16),
        in_specs=[pl.BlockSpec(memory_space=pl.ANY)] * len(blocks) + [vmem],
        out_specs=vmem,
        scratch_shapes=[
            pltpu.VMEM((rows, D), jnp.bfloat16),
            pltpu.SemaphoreType.DMA((len(blocks),)),
        ],
        compiler_params=pltpu.CompilerParams(vmem_limit_bytes=24 * MIB),
        cost_estimate=pl.CostEstimate(
            flops=6 * rows * D * HD, bytes_accessed=2 * rows * D, transcendentals=0
        ),
    )(*blocks, weight)


def attend_kernel(short, ready, place, *refs):
    *blocks, weight_ref, out_ref, rows_ref, qkv_ref, sems = refs
    blocks, done = blocks[ready:], blocks[:ready]
    start = 0
    for part in done:
        qkv_ref[start : start + part.shape[0], :] = part[...]
        start += part.shape[0]
    qkv_ref[start:, :] = project_rows(blocks, weight_ref, rows_ref, sems)
    factor = math.log2(math.e) / math.sqrt(HD)
    x, core, z, y = place[0], place[1], place[2], place[3]
    keys = qkv_ref[:, HD : 2 * HD]
    values = qkv_ref[:, 2 * HD :]
    places = places_short() if short else places_long()
    size = 256
    for b in range(TOKENS // size):
        query = qkv_ref[b * size : (b + 1) * size, :HD]
        scores = lax.dot_general(
            query, keys, (((1,), (1,)), ((), ())), preferred_element_type=jnp.float32
        )
        peak = jnp.max(scores, axis=-1, keepdims=True)
        expo = jnp.exp2((scores - peak) * factor)
        total = jnp.sum(expo, axis=-1, keepdims=True)
        mixed = jnp.dot(expo.astype(jnp.bfloat16), values, preferred_element_type=jnp.float32)
        mixed = (mixed / total).astype(jnp.bfloat16)
        for r in range(size // HALF):
            far, dy, half, other = places[b * (size // HALF) + r]
            owner = 1 - core if other else core
            sign = 1 - 2 * owner
            row = lax.rem(y + sign * dy + 4, 4)
            if short:
                slot = (2 * lax.rem(x + sign * far + 4, 4) + owner) * 4 + row
            else:
                slot = lax.rem(z + sign * far + 8, 8) * 4 + row
            out_ref[slot, half * HALF : (half + 1) * HALF, :] = mixed[r * HALF : (r + 1) * HALF]


def attend(place, done, blocks, weight, short):
    rows = sum(b.shape[0] for b in blocks)
    vmem = pl.BlockSpec(memory_space=pltpu.VMEM)
    return pl.pallas_call(
        functools.partial(attend_kernel, short, len(done)),
        out_shape=jax.ShapeDtypeStruct((TOKENS // 32, 32, HD), jnp.bfloat16),
        in_specs=[pl.BlockSpec(memory_space=pltpu.SMEM)]
        + [vmem] * len(done)
        + [pl.BlockSpec(memory_space=pl.ANY)] * len(blocks)
        + [vmem],
        out_specs=vmem,
        scratch_shapes=[
            pltpu.VMEM((rows, D), jnp.bfloat16),
            pltpu.VMEM((TOKENS, 3 * HD), jnp.bfloat16),
            pltpu.SemaphoreType.DMA((len(blocks),)),
        ],
        compiler_params=pltpu.CompilerParams(vmem_limit_bytes=32 * MIB),
        cost_estimate=pl.CostEstimate(
            flops=4 * TOKENS * TOKENS * HD + 6 * rows * D * HD,
            bytes_accessed=2 * rows * D,
            transcendentals=TOKENS * TOKENS,
        ),
    )(place, *done, *blocks, weight)


def weight_kernel(weight_ref, out_ref):
    for c in range(3):
        out_ref[:, c * HD : (c + 1) * HD] = weight_ref[c]


def side_by_side(weight):
    return pl.pallas_call(
        weight_kernel,
        out_shape=jax.ShapeDtypeStruct((D, 3 * HD), jnp.bfloat16),
        compiler_params=pltpu.CompilerParams(vmem_limit_bytes=16 * MIB),
        cost_estimate=pl.CostEstimate(flops=0, bytes_accessed=12 * D * HD, transcendentals=0),
    )(weight)


def norm(values):
    center = jnp.mean(values, axis=-1, keepdims=True)
    moved = values - center
    spread = jnp.mean(moved * moved, axis=-1, keepdims=True)
    return moved * lax.rsqrt(spread + 1e-05)


def norm_kernel(rows_ref, first_ref, second_ref):
    for n, out_ref in enumerate((first_ref, second_ref)):
        out_ref[...] = norm(rows_ref[n * HALF : (n + 1) * HALF, :]).astype(jnp.bfloat16)


def layer_norm(rows):
    half = jax.ShapeDtypeStruct((HALF, D), jnp.bfloat16)
    return pl.pallas_call(norm_kernel, out_shape=[half, half])(rows)


def sweep_kernel(width, attended_ref, anchor_ref, current_ref, out_ref, gap_ref, *updated_ref):
    anchor = anchor_ref[0]
    before = jnp.zeros_like(anchor)
    gap = jnp.zeros_like(anchor)
    for k in range(STEPS):
        current = current_ref[k]
        increment = width[k] * (attended_ref[k].astype(jnp.float32) - current)
        updated = anchor + before
        change = updated - current
        gap = gap + change * change
        if updated_ref:
            updated_ref[0][k] = updated
            out_ref[k] = norm(updated).astype(jnp.bfloat16)
        else:
            out_ref[k] = updated + increment
        before = before + increment
    gap_ref[...] = jnp.broadcast_to(jnp.sum(gap), gap_ref.shape)


def sweep_update(width, attended, anchor, current, last):
    shape = current.shape
    vmem = pl.BlockSpec(memory_space=pltpu.VMEM)
    outs = [
        jax.ShapeDtypeStruct(shape, jnp.float32 if last else jnp.bfloat16),
        jax.ShapeDtypeStruct((1, 128), jnp.float32),
    ]
    if not last:
        outs.append(jax.ShapeDtypeStruct(shape, jnp.float32))
    return pl.pallas_call(
        sweep_kernel,
        out_shape=outs,
        in_specs=[pl.BlockSpec(memory_space=pltpu.SMEM)] + [vmem] * 3,
        out_specs=[vmem] * len(outs),
    )(width, attended, anchor, current)


def over_step(pieces):
    return lax.all_to_all(pieces, STEP, split_axis=0, concat_axis=0, tiled=True)


def over_all(pieces):
    return lax.all_to_all(pieces, ALL, split_axis=0, concat_axis=0, tiled=True)


def deliver_kernel(place, own_ref, *refs):
    *pieces, out_ref = refs
    x, core = place[0], place[1]
    out_ref[2 * x + core] = own_ref[...]
    for n, piece in enumerate(pieces):
        far, flip = (n + 1) // 2, (n + 1) % 2
        out_ref[2 * lax.rem(x - far + 4, 4) + lax.rem(core + flip, 2)] = piece[...]


def deliver(place, pieces):
    x, core = place[0], place[1]
    got = []
    for n in range(8):
        far, flip = n // 2, n % 2
        target = 2 * lax.rem(x + far, 4) + lax.rem(core + flip, 2)
        piece = lax.dynamic_index_in_dim(pieces, target, 0, keepdims=False)
        if n:
            pairs = [
                (2 * i + c, 2 * ((i + far) % 4) + (c + flip) % 2) for i in range(4) for c in range(2)
            ]
            piece = lax.ppermute(piece, STEP, pairs)
        got.append(piece)
    vmem = pl.BlockSpec(memory_space=pltpu.VMEM)
    return pl.pallas_call(
        deliver_kernel,
        out_shape=jax.ShapeDtypeStruct(pieces.shape, pieces.dtype),
        in_specs=[pl.BlockSpec(memory_space=pltpu.SMEM)] + [vmem] * 8,
        out_specs=vmem,
    )(place, *got)


def local(step_index, window_init, qkv_weight):
    window = window_init[0]
    place = jnp.stack([lax.axis_index(a) for a in ALL]).astype(jnp.int32)
    width = (step_index[:-1] - step_index[1:]).astype(jnp.float32) / 1000.0
    weight = side_by_side(qkv_weight)
    wanted = lax.axis_index(STEP) == lax.axis_index("z")
    other_weight = lax.psum(jnp.where(wanted, weight, jnp.zeros_like(weight)), "z")

    groups, start = gather_long(*layer_norm(window), window)
    done = [project(group, weight) for group in groups[:-1]]
    attended = attend(place, done, groups[-1], weight, False)
    pieces = attended.reshape(32, STEPS, 4, HD).transpose(1, 0, 2, 3)
    got = over_all(pieces.reshape(256, 4, HD)).reshape(STEPS, HEADS, 4, HD)
    attended = got.transpose(0, 2, 1, 3).reshape(STEPS, 4, D)
    normed, first_gap, updated = sweep_update(width, attended, start[:1], start, False)

    rows = lax.all_to_all(normed, "z", split_axis=0, concat_axis=0, tiled=True).reshape(32, D)
    groups, other_weight = gather_short(rows, other_weight)
    done = [project(group, other_weight) for group in groups[:-1]]
    attended = attend(place, done, groups[-1], other_weight, True)
    pieces = attended.reshape(STEPS, 4, 8, 4, HD).transpose(0, 2, 1, 3, 4)
    got = over_all(pieces.reshape(256, 4, HD)).reshape(8, STEPS, 4, 4, HD)
    attended = got.transpose(1, 3, 0, 2, 4).reshape(STEPS, 4, D)
    advanced, second_gap = sweep_update(width, attended, start[:1], updated, True)
    marks = jnp.concatenate([first_gap, second_gap])[None]
    totals = jnp.sum(over_all(jnp.broadcast_to(marks, (256, 2, 128))), axis=0)[:, 0]
    residuals = jnp.sqrt(totals / (STEPS * TOKENS * D))
    return (deliver(place, advanced).reshape(1, 32, D), residuals)


def solution(mesh):
    fine = Mesh(mesh.devices.reshape(4, 2, 8, 4), ALL)
    placed = (P(), P(STEP, SEQ, None), P(None, None, SEQ))
    return jax.shard_map(
        local, mesh=fine, in_specs=placed, out_specs=(P(STEP, SEQ, None), P()), check_vma=False
    )
```

```python
import functools
import math

import jax
import jax.numpy as jnp
from jax import lax
from jax.experimental import pallas as pl
from jax.experimental.pallas import tpu as pltpu
from jax.sharding import Mesh, PartitionSpec as P

HD = 128
HEADS = 32
D = HEADS * HD
STEPS = 8
TOKENS = 1024
SIZES = {"x": 4, "c": 2, "z": 8, "y": 4}
STEP = ("x", "c")
SEQ = ("z", "y")
ALL = STEP + SEQ
HALF = 16
MIB = 1024 * 1024


def shift(x, axis, by):
    n = SIZES[axis]
    pairs = []
    for i in range(n):
        if axis == "x":
            pairs += [(2 * i, 2 * ((i + by) % n)), (2 * i + 1, 2 * ((i - by) % n) + 1)]
        else:
            pairs += [(i, (i + by) % n), (n + i, n + (i - by) % n)]
    return lax.ppermute(x, ("x", "c") if axis == "x" else ("c", axis), pairs)


def swap(x):
    return lax.ppermute(x, "c", [(0, 1), (1, 0)])


def join_kernel(*refs):
    *blocks, out_ref = refs
    start = 0
    for block in blocks:
        out_ref[start : start + block.shape[0], :] = block[...]
        start += block.shape[0]


def join(blocks):
    rows = sum(b.shape[0] for b in blocks)
    return pl.pallas_call(
        join_kernel,
        out_shape=jax.ShapeDtypeStruct((rows, D), jnp.bfloat16),
        in_specs=[pl.BlockSpec(memory_space=pltpu.VMEM)] * len(blocks),
        out_specs=pl.BlockSpec(memory_space=pltpu.VMEM),
        compiler_params=pltpu.CompilerParams(vmem_limit_bytes=8 * MIB),
        cost_estimate=pl.CostEstimate(flops=0, bytes_accessed=4 * rows * D, transcendentals=0),
    )(*blocks)


SMALL_4 = (0, -1, 1, -2)
SMALL_Z = (0, -4, -1, -5, 1, -3, 2, -2)


def small_4(x, axis):
    return join([x, shift(x, axis, 1), shift(x, axis, -1), shift(x, axis, 2)])


def small_z(x):
    pair = join([x, shift(x, "z", 4)])
    return join([pair, shift(pair, "z", 1), shift(pair, "z", -1), shift(pair, "z", -2)])


def tie(*values):
    return lax.optimization_barrier(values)


def ring_of_4(x, axis):
    up = shift(x, axis, 1)
    return {0: x, -1: up, 1: shift(x, axis, -1), -2: shift(up, axis, 1)}


LONG = (
    ((0, -1, 1), (0,)),
    ((-2, 2), (-1, 1)),
    ((-3, 3, -4), (-2,)),
)


def gather_long(first, second, window, masked):
    by_z = {0: small_4(first, "y")}
    by_z[0], second = tie(by_z[0], second)
    by_z[-1], by_z[1] = tie(shift(by_z[0], "z", 1), shift(by_z[0], "z", -1))
    by_y = ring_of_4(small_z(second), "y")
    by_z[-2], by_z[2] = tie(shift(by_z[-1], "z", 1), shift(by_z[1], "z", -1))
    by_z[-3], by_z[3] = shift(by_z[-2], "z", 1), shift(by_z[2], "z", -1)
    _, window = tie(by_z[-2], window)
    window = over_step(window.reshape(STEPS, 4, D))
    by_z[-4], masked = tie(shift(by_z[-3], "z", 1), masked)
    return [[by_z[d] for d in zs] + [by_y[d] for d in ys] for zs, ys in LONG], window, masked


def places_long():
    places = []
    for far_z, far_y in LONG:
        places += [(dz, dy, 0, 0) for dz in far_z for dy in SMALL_4]
        places += [(dz, dy, 1, 0) for dy in far_y for dz in SMALL_Z]
    return places


SHORT = ((0, -1, 1), (-2,))


def gather_short(x, weight):
    near_y, near_x = small_4(x[:HALF], "y"), small_4(x[HALF:], "x")
    near_y, near_x, weight = tie(near_y, near_x, weight)
    by_x, by_y = ring_of_4(near_y, "x"), ring_of_4(near_x, "y")
    groups = [[by_x[d] for d in far] + [by_y[d] for d in far] for far in SHORT]
    return [group + [swap(b) for b in group] for group in groups], weight


def places_short():
    places = []
    for far in SHORT:
        for core in (0, 1):
            places += [(dx, dy, 0, core) for dx in far for dy in SMALL_4]
            places += [(dx, dy, 1, core) for dy in far for dx in SMALL_4]
    return places


def project_rows(blocks, weight_any, weight_ref, rows_ref, sems):
    copies = [pltpu.make_async_copy(weight_any, weight_ref, sems.at[len(blocks)])]
    copies[0].start()
    start = 0
    for n, block in enumerate(blocks):
        rows = block.shape[0]
        copies.append(
            pltpu.make_async_copy(block, rows_ref.at[pl.ds(start, rows), :], sems.at[n])
        )
        copies[-1].start()
        start += rows
    for copy in copies:
        copy.wait()
    out = jnp.dot(rows_ref[...], weight_ref[...], preferred_element_type=jnp.float32)
    return out.astype(jnp.bfloat16)


def project_kernel(*refs):
    *blocks, weight_any, out_ref, weight_ref, rows_ref, sems = refs
    out_ref[...] = project_rows(blocks, weight_any, weight_ref, rows_ref, sems)


def project(blocks, weight, limit):
    rows = sum(b.shape[0] for b in blocks)
    return pl.pallas_call(
        project_kernel,
        out_shape=jax.ShapeDtypeStruct((rows, 3 * HD), jnp.bfloat16),
        in_specs=[pl.BlockSpec(memory_space=pl.ANY)] * (len(blocks) + 1),
        out_specs=pl.BlockSpec(memory_space=pltpu.VMEM),
        scratch_shapes=[
            pltpu.VMEM((D, 3 * HD), jnp.bfloat16),
            pltpu.VMEM((rows, D), jnp.bfloat16),
            pltpu.SemaphoreType.DMA((len(blocks) + 1,)),
        ],
        compiler_params=pltpu.CompilerParams(vmem_limit_bytes=limit),
        cost_estimate=pl.CostEstimate(
            flops=6 * rows * D * HD, bytes_accessed=2 * rows * D, transcendentals=0
        ),
    )(*blocks, weight)


def attend_kernel(short, ready, place, *refs):
    *blocks, weight_any, out_ref, weight_ref, rows_ref, qkv_ref, sems = refs
    blocks, done = blocks[ready:], blocks[:ready]
    start = 0
    for part in done:
        qkv_ref[start : start + part.shape[0], :] = part[...]
        start += part.shape[0]
    qkv_ref[start:, :] = project_rows(blocks, weight_any, weight_ref, rows_ref, sems)
    factor = math.log2(math.e) / math.sqrt(HD)
    x, core, z, y = place[0], place[1], place[2], place[3]
    keys = qkv_ref[:, HD : 2 * HD]
    values = qkv_ref[:, 2 * HD :]
    places = places_short() if short else places_long()
    size = 256
    for b in range(TOKENS // size):
        query = qkv_ref[b * size : (b + 1) * size, :HD]
        scores = lax.dot_general(
            query, keys, (((1,), (1,)), ((), ())), preferred_element_type=jnp.float32
        )
        peak = jnp.max(scores, axis=-1, keepdims=True)
        expo = jnp.exp2((scores - peak) * factor)
        total = jnp.sum(expo, axis=-1, keepdims=True)
        mixed = jnp.dot(expo.astype(jnp.bfloat16), values, preferred_element_type=jnp.float32)
        mixed = (mixed / total).astype(jnp.bfloat16)
        for r in range(size // HALF):
            far, dy, half, other = places[b * (size // HALF) + r]
            owner = 1 - core if other else core
            sign = 1 - 2 * owner
            row = lax.rem(y + sign * dy + 4, 4)
            if short:
                slot = (2 * lax.rem(x + sign * far + 4, 4) + owner) * 4 + row
            else:
                slot = lax.rem(z + sign * far + 8, 8) * 4 + row
            out_ref[slot, half * HALF : (half + 1) * HALF, :] = mixed[r * HALF : (r + 1) * HALF]


def attend(place, done, blocks, weight, short, limit):
    rows = sum(b.shape[0] for b in blocks)
    vmem = pl.BlockSpec(memory_space=pltpu.VMEM)
    return pl.pallas_call(
        functools.partial(attend_kernel, short, len(done)),
        out_shape=jax.ShapeDtypeStruct((TOKENS // 32, 32, HD), jnp.bfloat16),
        in_specs=[pl.BlockSpec(memory_space=pltpu.SMEM)]
        + [vmem] * len(done)
        + [pl.BlockSpec(memory_space=pl.ANY)] * (len(blocks) + 1),
        out_specs=vmem,
        scratch_shapes=[
            pltpu.VMEM((D, 3 * HD), jnp.bfloat16),
            pltpu.VMEM((rows, D), jnp.bfloat16),
            pltpu.VMEM((TOKENS, 3 * HD), jnp.bfloat16),
            pltpu.SemaphoreType.DMA((len(blocks) + 1,)),
        ],
        compiler_params=pltpu.CompilerParams(vmem_limit_bytes=limit),
        cost_estimate=pl.CostEstimate(
            flops=4 * TOKENS * TOKENS * HD + 6 * rows * D * HD,
            bytes_accessed=2 * rows * D,
            transcendentals=TOKENS * TOKENS,
        ),
    )(place, *done, *blocks, weight)


def weight_kernel(place, weight_ref, out_ref, masked_ref):
    wanted = 2 * place[0] + place[1] == place[2]
    for c in range(3):
        part = weight_ref[c]
        out_ref[:, c * HD : (c + 1) * HD] = part
        masked_ref[:, c * HD : (c + 1) * HD] = jnp.where(wanted, part, jnp.zeros_like(part))


def side_by_side(place, weight):
    out = jax.ShapeDtypeStruct((D, 3 * HD), jnp.bfloat16)
    vmem = pl.BlockSpec(memory_space=pltpu.VMEM)
    return pl.pallas_call(
        weight_kernel,
        out_shape=[out, out],
        in_specs=[pl.BlockSpec(memory_space=pltpu.SMEM), vmem],
        out_specs=[vmem, vmem],
        compiler_params=pltpu.CompilerParams(vmem_limit_bytes=16 * MIB),
        cost_estimate=pl.CostEstimate(flops=0, bytes_accessed=18 * D * HD, transcendentals=0),
    )(place, weight)


def norm(values):
    center = jnp.mean(values, axis=-1, keepdims=True)
    moved = values - center
    spread = jnp.mean(moved * moved, axis=-1, keepdims=True)
    return moved * lax.rsqrt(spread + 1e-05)


def norm_kernel(rows_ref, first_ref, second_ref):
    for n, out_ref in enumerate((first_ref, second_ref)):
        out_ref[...] = norm(rows_ref[n * HALF : (n + 1) * HALF, :]).astype(jnp.bfloat16)


def layer_norm(rows):
    half = jax.ShapeDtypeStruct((HALF, D), jnp.bfloat16)
    return pl.pallas_call(norm_kernel, out_shape=[half, half])(rows)


def sweep_steps(width, attended_ref, current_ref, store):
    anchor = current_ref[0]
    before = jnp.zeros_like(anchor)
    gap = jnp.zeros_like(anchor)
    for k in range(STEPS):
        current = current_ref[k]
        increment = width[k] * (attended_ref[k].astype(jnp.float32) - current)
        updated = anchor + before
        change = updated - current
        gap = gap + change * change
        store(k, updated, increment)
        before = before + increment
    return jnp.sum(gap)


def sweep_kernel(width, attended_ref, current_ref, normed_ref, gap_ref, updated_ref):
    def store(k, updated, increment):
        updated_ref[k] = updated
        normed_ref[k] = norm(updated).astype(jnp.bfloat16)

    gap = sweep_steps(width, attended_ref, current_ref, store)
    gap_ref[...] = jnp.broadcast_to(gap, gap_ref.shape)


def sweep_update(width, attended, current):
    shape = current.shape
    vmem = pl.BlockSpec(memory_space=pltpu.VMEM)
    return pl.pallas_call(
        sweep_kernel,
        out_shape=[
            jax.ShapeDtypeStruct(shape, jnp.bfloat16),
            jax.ShapeDtypeStruct((1, 1, 128), jnp.float32),
            jax.ShapeDtypeStruct(shape, jnp.float32),
        ],
        in_specs=[pl.BlockSpec(memory_space=pltpu.SMEM)] + [vmem] * 2,
        out_specs=[vmem] * 3,
    )(width, attended, current)


def step_pair(place, far, flip):
    return 2 * lax.rem(place[0] + far, 4) + lax.rem(place[1] + flip, 2)


def last_kernel(width, place, attended_ref, current_ref, first_ref, *refs):
    *piece_refs, marks_ref, advanced_ref = refs

    def store(k, updated, increment):
        advanced_ref[k] = updated + increment

    gap = sweep_steps(width, attended_ref, current_ref, store)
    for n, piece_ref in enumerate(piece_refs):
        piece_ref[...] = advanced_ref[step_pair(place, n // 2, n % 2)]
    marks_ref[:, 0:1, :] = jnp.broadcast_to(first_ref[...], (256, 1, 128))
    marks_ref[:, 1:2, :] = jnp.broadcast_to(gap, (256, 1, 128))


def last_update(width, place, attended, current, first_gap):
    vmem = pl.BlockSpec(memory_space=pltpu.VMEM)
    smem = pl.BlockSpec(memory_space=pltpu.SMEM)
    *pieces, marks = pl.pallas_call(
        last_kernel,
        out_shape=[jax.ShapeDtypeStruct(current.shape[1:], jnp.float32)] * STEPS
        + [jax.ShapeDtypeStruct((256, 2, 128), jnp.float32)],
        in_specs=[smem, smem] + [vmem] * 3,
        out_specs=[vmem] * (STEPS + 1),
        scratch_shapes=[pltpu.VMEM(current.shape, jnp.float32)],
    )(width, place, attended, current, first_gap)
    return pieces, marks


def over_step(pieces):
    return lax.all_to_all(pieces, STEP, split_axis=0, concat_axis=0, tiled=True)


def over_all(pieces):
    return lax.all_to_all(pieces, ALL, split_axis=0, concat_axis=0, tiled=True)


def deliver_kernel(place, *refs):
    *pieces, out_ref = refs
    swapped = place[1] == 1
    for far in range(4):
        same, other = pieces[2 * far][...], pieces[2 * far + 1][...]
        low = jnp.where(swapped, other, same)
        high = jnp.where(swapped, same, other)
        x = lax.rem(place[0] - far + 4, 4)
        out_ref[pl.ds(pl.multiple_of(8 * x, 8), 8), :] = jnp.concatenate([low, high], axis=0)


def deliver(place, pieces):
    got = pieces[:1]
    for n in range(1, STEPS):
        pairs = [
            (2 * i + c, 2 * ((i + n // 2) % 4) + (c + n) % 2) for i in range(4) for c in range(2)
        ]
        got.append(lax.ppermute(pieces[n], STEP, pairs))
    vmem = pl.BlockSpec(memory_space=pltpu.VMEM)
    return pl.pallas_call(
        deliver_kernel,
        out_shape=jax.ShapeDtypeStruct((32, D), jnp.float32),
        in_specs=[pl.BlockSpec(memory_space=pltpu.SMEM)] + [vmem] * STEPS,
        out_specs=vmem,
    )(place, *got)


def local(step_index, window_init, qkv_weight):
    window = window_init[0]
    place = jnp.stack([lax.axis_index(a) for a in ALL]).astype(jnp.int32)
    width = (step_index[:-1] - step_index[1:]).astype(jnp.float32) / 1000.0
    weight, masked = side_by_side(place, qkv_weight)

    groups, start, masked = gather_long(*layer_norm(window), window, masked)
    other_weight = lax.psum(masked, "z")
    done = [project(group, weight, 56 * MIB) for group in groups[:-1]]
    groups[-1][-1], start = tie(groups[-1][-1], start)
    attended = attend(place, done, groups[-1], weight, False, 56 * MIB)
    pieces = attended.reshape(32, STEPS, 4, HD).transpose(1, 0, 2, 3)
    got = over_all(pieces.reshape(256, 4, HD)).reshape(STEPS, HEADS, 4, HD)
    attended = got.transpose(0, 2, 1, 3).reshape(STEPS, 4, D)
    normed, first_gap, updated = sweep_update(width, attended, start)

    rows = lax.all_to_all(normed, "z", split_axis=0, concat_axis=0, tiled=True).reshape(32, D)
    groups, other_weight = gather_short(rows, other_weight)
    done = [project(group, other_weight, 16 * MIB) for group in groups[:-1]]
    attended = attend(place, done, groups[-1], other_weight, True, 20 * MIB)
    pieces = attended.reshape(STEPS, 4, 8, 4, HD).transpose(0, 2, 1, 3, 4)
    got = over_all(pieces.reshape(256, 4, HD)).reshape(8, STEPS, 4, 4, HD)
    attended = got.transpose(1, 3, 0, 2, 4).reshape(STEPS, 4, D)
    pieces, marks = last_update(width, place, attended, updated, first_gap)
    totals = jnp.sum(over_all(marks), axis=0)[:, 0]
    residuals = jnp.sqrt(totals / (STEPS * TOKENS * D))
    return (deliver(place, pieces)[None], residuals)


def solution(mesh):
    fine = Mesh(mesh.devices.reshape(4, 2, 8, 4), ALL)
    placed = (P(), P(STEP, SEQ, None), P(None, None, SEQ))
    return jax.shard_map(
        local, mesh=fine, in_specs=placed, out_specs=(P(STEP, SEQ, None), P()), check_vma=False
    )
```

```python
import functools
import math

import jax
import jax.numpy as jnp
from jax import lax
from jax.experimental import pallas as pl
from jax.experimental.pallas import tpu as pltpu
from jax.sharding import Mesh, PartitionSpec as P

HD = 128
HEADS = 32
D = HEADS * HD
STEPS = 8
TOKENS = 1024
SIZES = {"x": 4, "c": 2, "z": 8, "y": 4}
STEP = ("x", "c")
SEQ = ("z", "y")
ALL = STEP + SEQ
HALF = 16
MIB = 1024 * 1024


def shift(x, axis, by):
    n = SIZES[axis]
    pairs = []
    for i in range(n):
        if axis == "x":
            pairs += [(2 * i, 2 * ((i + by) % n)), (2 * i + 1, 2 * ((i - by) % n) + 1)]
        else:
            pairs += [(i, (i + by) % n), (n + i, n + (i - by) % n)]
    return lax.ppermute(x, ("x", "c") if axis == "x" else ("c", axis), pairs)


def swap(x):
    return lax.ppermute(x, "c", [(0, 1), (1, 0)])


def join_kernel(*refs):
    *blocks, out_ref = refs
    start = 0
    for block in blocks:
        out_ref[start : start + block.shape[0], :] = block[...]
        start += block.shape[0]


def join(blocks):
    rows = sum(b.shape[0] for b in blocks)
    return pl.pallas_call(
        join_kernel,
        out_shape=jax.ShapeDtypeStruct((rows, D), jnp.bfloat16),
        in_specs=[pl.BlockSpec(memory_space=pltpu.VMEM)] * len(blocks),
        out_specs=pl.BlockSpec(memory_space=pltpu.VMEM),
        compiler_params=pltpu.CompilerParams(vmem_limit_bytes=8 * MIB),
        cost_estimate=pl.CostEstimate(flops=0, bytes_accessed=4 * rows * D, transcendentals=0),
    )(*blocks)


SMALL_4 = (0, -1, 1, -2)
SMALL_Z = (0, -4, -1, -5, 1, -3, 2, -2)


def small_4(x, axis):
    return join([x, shift(x, axis, 1), shift(x, axis, -1), shift(x, axis, 2)])


def small_z(x):
    pair = join([x, shift(x, "z", 4)])
    return join([pair, shift(pair, "z", 1), shift(pair, "z", -1), shift(pair, "z", -2)])


def tie(*values):
    return lax.optimization_barrier(values)


def both_ways(up, down, axis):
    return tie(shift(up, axis, 1), shift(down, axis, -1))


def ring_of_4(x, axis):
    up, down = both_ways(x, x, axis)
    return {0: x, -1: up, 1: down, -2: shift(up, axis, 1)}


LONG = (
    ((0, -1, 1), (0,)),
    ((-2, 2), (-1, 1)),
    ((-3, 3, -4), (-2,)),
)


def gather_long(first, second, window, weights):
    by_z = {0: small_4(first, "y")}
    up, down = both_ways(by_z[0], by_z[0], "z")
    near_z = small_z(second)
    up, down, weight, masked = tie(up, down, *weights)
    by_z[-1], by_z[1] = up, down
    by_y = ring_of_4(near_z, "y")
    by_z[-2], by_z[2] = both_ways(up, down, "z")
    _, window = tie(by_z[-2], window)
    window = over_step(window.reshape(STEPS, 4, D))
    by_z[-3], by_z[3] = both_ways(by_z[-2], by_z[2], "z")
    last, window = tie(by_z[-3], window)
    by_z[-4], masked = tie(shift(last, "z", 1), masked)
    groups = [[by_z[d] for d in zs] + [by_y[d] for d in ys] for zs, ys in LONG]
    return groups, window, weight, masked


def places_long():
    places = []
    for far_z, far_y in LONG:
        places += [(dz, dy, 0, 0) for dz in far_z for dy in SMALL_4]
        places += [(dz, dy, 1, 0) for dy in far_y for dz in SMALL_Z]
    return places


SHORT = ((0, -1, 1), (-2,))


def gather_short(x, weight):
    near_y, near_x = small_4(x[:HALF], "y"), small_4(x[HALF:], "x")
    near_y, near_x = tie(near_y, near_x)
    by_x, by_y = ring_of_4(near_y, "x"), ring_of_4(near_x, "y")
    by_x[-2], weight = tie(by_x[-2], weight)
    groups = [[by_x[d] for d in far] + [by_y[d] for d in far] for far in SHORT]
    return [group + [swap(b) for b in group] for group in groups], weight


def places_short():
    places = []
    for far in SHORT:
        for core in (0, 1):
            places += [(dx, dy, 0, core) for dx in far for dy in SMALL_4]
            places += [(dx, dy, 1, core) for dy in far for dx in SMALL_4]
    return places


def project_rows(blocks, weight_ref, rows_ref, sems):
    copies = []
    start = 0
    for n, block in enumerate(blocks):
        rows = block.shape[0]
        copies.append(
            pltpu.make_async_copy(block, rows_ref.at[pl.ds(start, rows), :], sems.at[n])
        )
        copies[-1].start()
        start += rows
    for copy in copies:
        copy.wait()
    out = jnp.dot(rows_ref[...], weight_ref[...], preferred_element_type=jnp.float32)
    return out.astype(jnp.bfloat16)


def project_kernel(*refs):
    *blocks, weight_ref, out_ref, rows_ref, sems = refs
    out_ref[...] = project_rows(blocks, weight_ref, rows_ref, sems)


def project(blocks, weight, limit):
    rows = sum(b.shape[0] for b in blocks)
    vmem = pl.BlockSpec(memory_space=pltpu.VMEM)
    return pl.pallas_call(
        project_kernel,
        out_shape=jax.ShapeDtypeStruct((rows, 3 * HD), jnp.bfloat16),
        in_specs=[pl.BlockSpec(memory_space=pl.ANY)] * len(blocks) + [vmem],
        out_specs=vmem,
        scratch_shapes=[
            pltpu.VMEM((rows, D), jnp.bfloat16),
            pltpu.SemaphoreType.DMA((len(blocks),)),
        ],
        compiler_params=pltpu.CompilerParams(vmem_limit_bytes=limit),
        cost_estimate=pl.CostEstimate(
            flops=6 * rows * D * HD, bytes_accessed=2 * rows * D, transcendentals=0
        ),
    )(*blocks, weight)


def attend_kernel(short, ready, place, *refs):
    *blocks, weight_ref, out_ref, rows_ref, qkv_ref, sems = refs
    blocks, done = blocks[ready:], blocks[:ready]
    start = 0
    for part in done:
        qkv_ref[start : start + part.shape[0], :] = part[...]
        start += part.shape[0]
    qkv_ref[start:, :] = project_rows(blocks, weight_ref, rows_ref, sems)
    factor = math.log2(math.e) / math.sqrt(HD)
    x, core, z, y = place[0], place[1], place[2], place[3]
    keys = qkv_ref[:, HD : 2 * HD]
    values = qkv_ref[:, 2 * HD :]
    places = places_short() if short else places_long()
    size = 256
    for b in range(TOKENS // size):
        query = qkv_ref[b * size : (b + 1) * size, :HD]
        scores = lax.dot_general(
            query, keys, (((1,), (1,)), ((), ())), preferred_element_type=jnp.float32
        )
        peak = jnp.max(scores, axis=-1, keepdims=True)
        expo = jnp.exp2((scores - peak) * factor)
        total = jnp.sum(expo, axis=-1, keepdims=True)
        mixed = jnp.dot(expo.astype(jnp.bfloat16), values, preferred_element_type=jnp.float32)
        mixed = (mixed / total).astype(jnp.bfloat16)
        for r in range(size // HALF):
            far, dy, half, other = places[b * (size // HALF) + r]
            owner = 1 - core if other else core
            sign = 1 - 2 * owner
            row = lax.rem(y + sign * dy + 4, 4)
            if short:
                slot = (2 * lax.rem(x + sign * far + 4, 4) + owner) * 4 + row
            else:
                slot = lax.rem(z + sign * far + 8, 8) * 4 + row
            out_ref[slot, half * HALF : (half + 1) * HALF, :] = mixed[r * HALF : (r + 1) * HALF]


def attend(place, done, blocks, weight, short, limit):
    rows = sum(b.shape[0] for b in blocks)
    vmem = pl.BlockSpec(memory_space=pltpu.VMEM)
    return pl.pallas_call(
        functools.partial(attend_kernel, short, len(done)),
        out_shape=jax.ShapeDtypeStruct((TOKENS // 32, 32, HD), jnp.bfloat16),
        in_specs=[pl.BlockSpec(memory_space=pltpu.SMEM)]
        + [vmem] * len(done)
        + [pl.BlockSpec(memory_space=pl.ANY)] * len(blocks)
        + [vmem],
        out_specs=vmem,
        scratch_shapes=[
            pltpu.VMEM((rows, D), jnp.bfloat16),
            pltpu.VMEM((TOKENS, 3 * HD), jnp.bfloat16),
            pltpu.SemaphoreType.DMA((len(blocks),)),
        ],
        compiler_params=pltpu.CompilerParams(vmem_limit_bytes=limit),
        cost_estimate=pl.CostEstimate(
            flops=4 * TOKENS * TOKENS * HD + 6 * rows * D * HD,
            bytes_accessed=2 * rows * D,
            transcendentals=TOKENS * TOKENS,
        ),
    )(place, *done, *blocks, weight)


def weight_kernel(place, weight_ref, out_ref, masked_ref):
    wanted = 2 * place[0] + place[1] == place[2]
    for c in range(3):
        part = weight_ref[c]
        out_ref[:, c * HD : (c + 1) * HD] = part
        masked_ref[:, c * HD : (c + 1) * HD] = jnp.where(wanted, part, jnp.zeros_like(part))


def side_by_side(place, weight):
    out = jax.ShapeDtypeStruct((D, 3 * HD), jnp.bfloat16)
    vmem = pl.BlockSpec(memory_space=pltpu.VMEM)
    return pl.pallas_call(
        weight_kernel,
        out_shape=[out, out],
        in_specs=[pl.BlockSpec(memory_space=pltpu.SMEM), vmem],
        out_specs=[vmem, vmem],
        compiler_params=pltpu.CompilerParams(vmem_limit_bytes=16 * MIB),
        cost_estimate=pl.CostEstimate(flops=0, bytes_accessed=18 * D * HD, transcendentals=0),
    )(place, weight)


def norm(values):
    center = jnp.mean(values, axis=-1, keepdims=True)
    moved = values - center
    spread = jnp.mean(moved * moved, axis=-1, keepdims=True)
    return moved * lax.rsqrt(spread + 1e-05)


def norm_kernel(rows_ref, first_ref, second_ref):
    for n, out_ref in enumerate((first_ref, second_ref)):
        out_ref[...] = norm(rows_ref[n * HALF : (n + 1) * HALF, :]).astype(jnp.bfloat16)


def layer_norm(rows):
    half = jax.ShapeDtypeStruct((HALF, D), jnp.bfloat16)
    return pl.pallas_call(norm_kernel, out_shape=[half, half])(rows)


def sweep_steps(width, attended_ref, current_ref, store):
    anchor = current_ref[0]
    before = jnp.zeros_like(anchor)
    gap = jnp.zeros_like(anchor)
    for k in range(STEPS):
        current = current_ref[k]
        increment = width[k] * (attended_ref[k].astype(jnp.float32) - current)
        updated = anchor + before
        change = updated - current
        gap = gap + change * change
        store(k, updated, increment)
        before = before + increment
    return jnp.sum(gap)


def sweep_kernel(width, attended_ref, current_ref, normed_ref, gap_ref, updated_ref):
    def store(k, updated, increment):
        updated_ref[k] = updated
        normed_ref[k] = norm(updated).astype(jnp.bfloat16)

    gap = sweep_steps(width, attended_ref, current_ref, store)
    gap_ref[...] = jnp.broadcast_to(gap, gap_ref.shape)


def sweep_update(width, attended, current):
    shape = current.shape
    vmem = pl.BlockSpec(memory_space=pltpu.VMEM)
    return pl.pallas_call(
        sweep_kernel,
        out_shape=[
            jax.ShapeDtypeStruct(shape, jnp.bfloat16),
            jax.ShapeDtypeStruct((1, 1, 128), jnp.float32),
            jax.ShapeDtypeStruct(shape, jnp.float32),
        ],
        in_specs=[pl.BlockSpec(memory_space=pltpu.SMEM)] + [vmem] * 2,
        out_specs=[vmem] * 3,
    )(width, attended, current)


def step_pair(place, far, flip):
    return 2 * lax.rem(place[0] + far, 4) + lax.rem(place[1] + flip, 2)


def last_kernel(width, place, attended_ref, current_ref, first_ref, *refs):
    *piece_refs, marks_ref, advanced_ref = refs

    def store(k, updated, increment):
        advanced_ref[k] = updated + increment

    gap = sweep_steps(width, attended_ref, current_ref, store)
    for n, piece_ref in enumerate(piece_refs):
        piece_ref[...] = advanced_ref[step_pair(place, n // 2, n % 2)]
    marks_ref[:, 0:1, :] = jnp.broadcast_to(first_ref[...], (256, 1, 128))
    marks_ref[:, 1:2, :] = jnp.broadcast_to(gap, (256, 1, 128))


def last_update(width, place, attended, current, first_gap):
    vmem = pl.BlockSpec(memory_space=pltpu.VMEM)
    smem = pl.BlockSpec(memory_space=pltpu.SMEM)
    *pieces, marks = pl.pallas_call(
        last_kernel,
        out_shape=[jax.ShapeDtypeStruct(current.shape[1:], jnp.float32)] * STEPS
        + [jax.ShapeDtypeStruct((256, 2, 128), jnp.float32)],
        in_specs=[smem, smem] + [vmem] * 3,
        out_specs=[vmem] * (STEPS + 1),
        scratch_shapes=[pltpu.VMEM(current.shape, jnp.float32)],
    )(width, place, attended, current, first_gap)
    return pieces, marks


def over_step(pieces):
    return lax.all_to_all(pieces, STEP, split_axis=0, concat_axis=0, tiled=True)


def over_all(pieces):
    return lax.all_to_all(pieces, ALL, split_axis=0, concat_axis=0, tiled=True)


def deliver_kernel(place, *refs):
    *pieces, out_ref = refs
    swapped = place[1] == 1
    for far in range(4):
        same, other = pieces[2 * far][...], pieces[2 * far + 1][...]
        low = jnp.where(swapped, other, same)
        high = jnp.where(swapped, same, other)
        x = lax.rem(place[0] - far + 4, 4)
        out_ref[pl.ds(pl.multiple_of(8 * x, 8), 8), :] = jnp.concatenate([low, high], axis=0)


def deliver(place, pieces):
    got = pieces[:1]
    for n in range(1, STEPS):
        pairs = [
            (2 * i + c, 2 * ((i + n // 2) % 4) + (c + n) % 2) for i in range(4) for c in range(2)
        ]
        got.append(lax.ppermute(pieces[n], STEP, pairs))
    vmem = pl.BlockSpec(memory_space=pltpu.VMEM)
    return pl.pallas_call(
        deliver_kernel,
        out_shape=jax.ShapeDtypeStruct((32, D), jnp.float32),
        in_specs=[pl.BlockSpec(memory_space=pltpu.SMEM)] + [vmem] * STEPS,
        out_specs=vmem,
    )(place, *got)


def local(step_index, window_init, qkv_weight):
    window = window_init[0]
    place = jnp.stack([lax.axis_index(a) for a in ALL]).astype(jnp.int32)
    width = (step_index[:-1] - step_index[1:]).astype(jnp.float32) / 1000.0
    weights = side_by_side(place, qkv_weight)
    groups, start, weight, masked = gather_long(*layer_norm(window), window, weights)
    other_weight = lax.psum(masked, "z")
    done = [project(group, weight, 24 * MIB) for group in groups[:-1]]
    attended = attend(place, done, groups[-1], weight, False, 24 * MIB)
    pieces = attended.reshape(32, STEPS, 4, HD).transpose(1, 0, 2, 3)
    got = over_all(pieces.reshape(256, 4, HD)).reshape(STEPS, HEADS, 4, HD)
    attended = got.transpose(0, 2, 1, 3).reshape(STEPS, 4, D)
    normed, first_gap, updated = sweep_update(width, attended, start)

    rows = lax.all_to_all(normed, "z", split_axis=0, concat_axis=0, tiled=True).reshape(32, D)
    groups, other_weight = gather_short(rows, other_weight)
    done = [project(group, other_weight, 24 * MIB) for group in groups[:-1]]
    attended = attend(place, done, groups[-1], other_weight, True, 24 * MIB)
    pieces = attended.reshape(STEPS, 4, 8, 4, HD).transpose(0, 2, 1, 3, 4)
    got = over_all(pieces.reshape(256, 4, HD)).reshape(8, STEPS, 4, 4, HD)
    attended = got.transpose(1, 3, 0, 2, 4).reshape(STEPS, 4, D)
    pieces, marks = last_update(width, place, attended, updated, first_gap)
    totals = jnp.sum(over_all(marks), axis=0)[:, 0]
    residuals = jnp.sqrt(totals / (STEPS * TOKENS * D))
    return (deliver(place, pieces)[None], residuals)


def solution(mesh):
    fine = Mesh(mesh.devices.reshape(4, 2, 8, 4), ALL)
    placed = (P(), P(STEP, SEQ, None), P(None, None, SEQ))
    return jax.shard_map(
        local, mesh=fine, in_specs=placed, out_specs=(P(STEP, SEQ, None), P()), check_vma=False
    )
```

```python
import functools
import math

import jax
import jax.numpy as jnp
from jax import lax
from jax.experimental import pallas as pl
from jax.experimental.pallas import tpu as pltpu
from jax.sharding import Mesh, PartitionSpec as P

HD = 128
HEADS = 32
D = HEADS * HD
STEPS = 8
TOKENS = 1024
SIZES = {"x": 4, "c": 2, "z": 8, "y": 4}
STEP = ("x", "c")
SEQ = ("z", "y")
ALL = STEP + SEQ
HALF = 16
MIB = 1024 * 1024


def shift(x, axis, by):
    n = SIZES[axis]
    pairs = []
    for i in range(n):
        if axis == "x":
            pairs += [(2 * i, 2 * ((i + by) % n)), (2 * i + 1, 2 * ((i - by) % n) + 1)]
        else:
            pairs += [(i, (i + by) % n), (n + i, n + (i - by) % n)]
    return lax.ppermute(x, ("x", "c") if axis == "x" else ("c", axis), pairs)


def swap(x):
    return lax.ppermute(x, "c", [(0, 1), (1, 0)])


def join_kernel(*refs):
    *blocks, out_ref = refs
    start = 0
    for block in blocks:
        out_ref[start : start + block.shape[0], :] = block[...]
        start += block.shape[0]


def join(blocks):
    rows = sum(b.shape[0] for b in blocks)
    return pl.pallas_call(
        join_kernel,
        out_shape=jax.ShapeDtypeStruct((rows, D), jnp.bfloat16),
        in_specs=[pl.BlockSpec(memory_space=pltpu.VMEM)] * len(blocks),
        out_specs=pl.BlockSpec(memory_space=pltpu.VMEM),
        compiler_params=pltpu.CompilerParams(vmem_limit_bytes=8 * MIB),
        cost_estimate=pl.CostEstimate(flops=0, bytes_accessed=4 * rows * D, transcendentals=0),
    )(*blocks)


SMALL_4 = (0, -1, 1, -2)
SMALL_Z = (0, -4, -1, -5, 1, -3, 2, -2)


def small_4(x, axis):
    return join([x, shift(x, axis, 1), shift(x, axis, -1), shift(x, axis, 2)])


def small_z(x):
    pair = join([x, shift(x, "z", 4)])
    return join([pair, shift(pair, "z", 1), shift(pair, "z", -1), shift(pair, "z", -2)])


def tie(*values):
    return lax.optimization_barrier(values)


def both_ways(up, down, axis):
    return tie(shift(up, axis, 1), shift(down, axis, -1))


def ring_of_4(x, axis):
    up, down = both_ways(x, x, axis)
    return {0: x, -1: up, 1: down, -2: shift(up, axis, 1)}


LONG = (
    ((0, -1, 1), (0,)),
    ((-2, 2), (-1, 1)),
    ((-3, 3, -4), (-2,)),
)


def gather_long(first, second, window, weight):
    by_z = {0: small_4(first, "y")}
    up, down = both_ways(by_z[0], by_z[0], "z")
    near_z = small_z(second)
    up, down, weight = tie(up, down, weight)
    by_z[-1], by_z[1] = up, down
    by_y = ring_of_4(near_z, "y")
    by_z[-2], by_z[2] = both_ways(up, down, "z")
    _, window = tie(by_z[-2], window)
    window = over_step(window.reshape(STEPS, 4, D))
    by_z[-3], by_z[3] = both_ways(by_z[-2], by_z[2], "z")
    by_z[-4] = shift(by_z[-3], "z", 1)
    groups = [[by_z[d] for d in zs] + [by_y[d] for d in ys] for zs, ys in LONG]
    groups[1][0], window = tie(groups[1][0], window)
    return groups, window, weight


def places_long():
    places = []
    for far_z, far_y in LONG:
        places += [(dz, dy, 0, 0) for dz in far_z for dy in SMALL_4]
        places += [(dz, dy, 1, 0) for dy in far_y for dz in SMALL_Z]
    return places


NEAR, FAR = (0, -1, 1), (-2,)


def gather_short(x):
    near_y, near_x = tie(small_4(x[:HALF], "y"), small_4(x[HALF:], "x"))
    by_x, by_y = ring_of_4(near_y, "x"), ring_of_4(near_x, "y")
    near = [by_x[d] for d in NEAR] + [by_y[d] for d in NEAR]
    far = [by_x[d] for d in FAR] + [by_y[d] for d in FAR]
    return [near, [swap(b) for b in near], far + [swap(b) for b in far]]


def places_short():
    places = []
    for far in (NEAR, FAR):
        for core in (0, 1):
            places += [(dx, dy, 0, core) for dx in far for dy in SMALL_4]
            places += [(dx, dy, 1, core) for dy in far for dx in SMALL_4]
    return places


def project_rows(blocks, weight_ref, rows_ref, sems):
    copies = []
    start = 0
    for n, block in enumerate(blocks):
        rows = block.shape[0]
        copies.append(
            pltpu.make_async_copy(block, rows_ref.at[pl.ds(start, rows), :], sems.at[n])
        )
        copies[-1].start()
        start += rows
    for copy in copies:
        copy.wait()
    out = jnp.dot(rows_ref[...], weight_ref[...], preferred_element_type=jnp.float32)
    return out.astype(jnp.bfloat16)


def project_kernel(*refs):
    *blocks, weight_ref, out_ref, rows_ref, sems = refs
    out_ref[...] = project_rows(blocks, weight_ref, rows_ref, sems)


def project(blocks, weight, limit):
    rows = sum(b.shape[0] for b in blocks)
    vmem = pl.BlockSpec(memory_space=pltpu.VMEM)
    return pl.pallas_call(
        project_kernel,
        out_shape=jax.ShapeDtypeStruct((rows, 3 * HD), jnp.bfloat16),
        in_specs=[pl.BlockSpec(memory_space=pl.ANY)] * len(blocks) + [vmem],
        out_specs=vmem,
        scratch_shapes=[
            pltpu.VMEM((rows, D), jnp.bfloat16),
            pltpu.SemaphoreType.DMA((len(blocks),)),
        ],
        compiler_params=pltpu.CompilerParams(vmem_limit_bytes=limit),
        cost_estimate=pl.CostEstimate(
            flops=6 * rows * D * HD, bytes_accessed=2 * rows * D, transcendentals=0
        ),
    )(*blocks, weight)


def attend_kernel(short, ready, place, *refs):
    *blocks, weight_ref, out_ref, rows_ref, qkv_ref, sems = refs
    blocks, done = blocks[ready:], blocks[:ready]
    start = 0
    for part in done:
        qkv_ref[start : start + part.shape[0], :] = part[...]
        start += part.shape[0]
    qkv_ref[start:, :] = project_rows(blocks, weight_ref, rows_ref, sems)
    factor = math.log2(math.e) / math.sqrt(HD)
    x, core, z, y = place[0], place[1], place[2], place[3]
    keys = qkv_ref[:, HD : 2 * HD]
    values = qkv_ref[:, 2 * HD :]
    places = places_short() if short else places_long()
    size = 256
    for b in range(TOKENS // size):
        query = qkv_ref[b * size : (b + 1) * size, :HD]
        scores = lax.dot_general(
            query, keys, (((1,), (1,)), ((), ())), preferred_element_type=jnp.float32
        )
        peak = jnp.max(scores, axis=-1, keepdims=True)
        expo = jnp.exp2((scores - peak) * factor)
        total = jnp.sum(expo, axis=-1, keepdims=True)
        mixed = jnp.dot(expo.astype(jnp.bfloat16), values, preferred_element_type=jnp.float32)
        mixed = (mixed / total).astype(jnp.bfloat16)
        for r in range(size // HALF):
            far, dy, half, other = places[b * (size // HALF) + r]
            owner = 1 - core if other else core
            sign = 1 - 2 * owner
            row = lax.rem(y + sign * dy + 4, 4)
            if short:
                slot = (2 * lax.rem(x + sign * far + 4, 4) + owner) * 4 + row
            else:
                slot = lax.rem(z + sign * far + 8, 8) * 4 + row
            out_ref[slot, half * HALF : (half + 1) * HALF, :] = mixed[r * HALF : (r + 1) * HALF]


def attend(place, done, blocks, weight, short, limit):
    rows = sum(b.shape[0] for b in blocks)
    vmem = pl.BlockSpec(memory_space=pltpu.VMEM)
    return pl.pallas_call(
        functools.partial(attend_kernel, short, len(done)),
        out_shape=jax.ShapeDtypeStruct((TOKENS // 32, 32, HD), jnp.bfloat16),
        in_specs=[pl.BlockSpec(memory_space=pltpu.SMEM)]
        + [vmem] * len(done)
        + [pl.BlockSpec(memory_space=pl.ANY)] * len(blocks)
        + [vmem],
        out_specs=vmem,
        scratch_shapes=[
            pltpu.VMEM((rows, D), jnp.bfloat16),
            pltpu.VMEM((TOKENS, 3 * HD), jnp.bfloat16),
            pltpu.SemaphoreType.DMA((len(blocks),)),
        ],
        compiler_params=pltpu.CompilerParams(vmem_limit_bytes=limit),
        cost_estimate=pl.CostEstimate(
            flops=4 * TOKENS * TOKENS * HD + 6 * rows * D * HD,
            bytes_accessed=2 * rows * D,
            transcendentals=TOKENS * TOKENS,
        ),
    )(place, *done, *blocks, weight)


def weight_kernel(weight_ref, out_ref):
    for c in range(3):
        out_ref[:, c * HD : (c + 1) * HD] = weight_ref[c]


def side_by_side(weight):
    vmem = pl.BlockSpec(memory_space=pltpu.VMEM)
    return pl.pallas_call(
        weight_kernel,
        out_shape=jax.ShapeDtypeStruct((D, 3 * HD), jnp.bfloat16),
        in_specs=[vmem],
        out_specs=vmem,
        compiler_params=pltpu.CompilerParams(vmem_limit_bytes=16 * MIB),
        cost_estimate=pl.CostEstimate(flops=0, bytes_accessed=12 * D * HD, transcendentals=0),
    )(weight)


def eighth_of_other(place, weight):
    rank = 2 * place[0] + place[1]
    part = lax.dynamic_slice_in_dim(weight, rank * (D // 8), D // 8, 0)
    pairs = [(r * 8 + z, z * 8 + r) for r in range(8) for z in range(8)]
    return lax.ppermute(part, ("x", "c", "z"), pairs)


def norm(values):
    center = jnp.mean(values, axis=-1, keepdims=True)
    moved = values - center
    spread = jnp.mean(moved * moved, axis=-1, keepdims=True)
    return moved * lax.rsqrt(spread + 1e-05)


def norm_kernel(rows_ref, first_ref, second_ref):
    for n, out_ref in enumerate((first_ref, second_ref)):
        out_ref[...] = norm(rows_ref[n * HALF : (n + 1) * HALF, :]).astype(jnp.bfloat16)


def layer_norm(rows):
    half = jax.ShapeDtypeStruct((HALF, D), jnp.bfloat16)
    return pl.pallas_call(norm_kernel, out_shape=[half, half])(rows)


def sweep_steps(width, attended_ref, current_ref, store):
    anchor = current_ref[0]
    before = jnp.zeros_like(anchor)
    gap = jnp.zeros_like(anchor)
    for k in range(STEPS):
        current = current_ref[k]
        increment = width[k] * (attended_ref[k].astype(jnp.float32) - current)
        updated = anchor + before
        change = updated - current
        gap = gap + change * change
        store(k, updated, increment)
        before = before + increment
    return jnp.sum(gap)


def sweep_kernel(width, attended_ref, current_ref, normed_ref, gap_ref, updated_ref):
    def store(k, updated, increment):
        updated_ref[k] = updated
        normed_ref[k] = norm(updated).astype(jnp.bfloat16)

    gap = sweep_steps(width, attended_ref, current_ref, store)
    gap_ref[...] = jnp.broadcast_to(gap, gap_ref.shape)


def sweep_update(width, attended, current):
    shape = current.shape
    vmem = pl.BlockSpec(memory_space=pltpu.VMEM)
    return pl.pallas_call(
        sweep_kernel,
        out_shape=[
            jax.ShapeDtypeStruct(shape, jnp.bfloat16),
            jax.ShapeDtypeStruct((1, 1, 128), jnp.float32),
            jax.ShapeDtypeStruct(shape, jnp.float32),
        ],
        in_specs=[pl.BlockSpec(memory_space=pltpu.SMEM)] + [vmem] * 2,
        out_specs=[vmem] * 3,
    )(width, attended, current)


def step_pair(place, far, flip):
    return 2 * lax.rem(place[0] + far, 4) + lax.rem(place[1] + flip, 2)


def last_kernel(width, place, attended_ref, current_ref, first_ref, *refs):
    *piece_refs, marks_ref, advanced_ref = refs

    def store(k, updated, increment):
        advanced_ref[k] = updated + increment

    gap = sweep_steps(width, attended_ref, current_ref, store)
    for n, piece_ref in enumerate(piece_refs):
        piece_ref[...] = advanced_ref[step_pair(place, n // 2, n % 2)]
    marks_ref[:, 0:1, :] = jnp.broadcast_to(first_ref[...], (256, 1, 128))
    marks_ref[:, 1:2, :] = jnp.broadcast_to(gap, (256, 1, 128))


def last_update(width, place, attended, current, first_gap):
    vmem = pl.BlockSpec(memory_space=pltpu.VMEM)
    smem = pl.BlockSpec(memory_space=pltpu.SMEM)
    *pieces, marks = pl.pallas_call(
        last_kernel,
        out_shape=[jax.ShapeDtypeStruct(current.shape[1:], jnp.float32)] * STEPS
        + [jax.ShapeDtypeStruct((256, 2, 128), jnp.float32)],
        in_specs=[smem, smem] + [vmem] * 3,
        out_specs=[vmem] * (STEPS + 1),
        scratch_shapes=[pltpu.VMEM(current.shape, jnp.float32)],
    )(width, place, attended, current, first_gap)
    return pieces, marks


def over_step(pieces):
    return lax.all_to_all(pieces, STEP, split_axis=0, concat_axis=0, tiled=True)


def over_all(pieces):
    return lax.all_to_all(pieces, ALL, split_axis=0, concat_axis=0, tiled=True)


def deliver_kernel(place, *refs):
    *pieces, out_ref = refs
    swapped = place[1] == 1
    for far in range(4):
        same, other = pieces[2 * far][...], pieces[2 * far + 1][...]
        low = jnp.where(swapped, other, same)
        high = jnp.where(swapped, same, other)
        x = lax.rem(place[0] - far + 4, 4)
        out_ref[pl.ds(pl.multiple_of(8 * x, 8), 8), :] = jnp.concatenate([low, high], axis=0)


def deliver(place, pieces):
    got = pieces[:1]
    for n in range(1, STEPS):
        pairs = [
            (2 * i + c, 2 * ((i + n // 2) % 4) + (c + n) % 2) for i in range(4) for c in range(2)
        ]
        got.append(lax.ppermute(pieces[n], STEP, pairs))
    vmem = pl.BlockSpec(memory_space=pltpu.VMEM)
    return pl.pallas_call(
        deliver_kernel,
        out_shape=jax.ShapeDtypeStruct((32, D), jnp.float32),
        in_specs=[pl.BlockSpec(memory_space=pltpu.SMEM)] + [vmem] * STEPS,
        out_specs=vmem,
    )(place, *got)


def local(step_index, window_init, qkv_weight):
    window = window_init[0]
    place = jnp.stack([lax.axis_index(a) for a in ALL]).astype(jnp.int32)
    width = (step_index[:-1] - step_index[1:]).astype(jnp.float32) / 1000.0
    weight = side_by_side(qkv_weight)
    groups, start, weight = gather_long(*layer_norm(window), window, weight)
    part = eighth_of_other(place, weight)
    done = [project(group, weight, 24 * MIB) for group in groups[:-1]]
    attended = attend(place, done, groups[-1], weight, False, 24 * MIB)
    pieces = attended.reshape(32, STEPS, 4, HD).transpose(1, 0, 2, 3)
    got, part = tie(over_all(pieces.reshape(256, 4, HD)), part)
    other_weight = lax.all_gather(part, "z", axis=0, tiled=True)
    got = got.reshape(STEPS, HEADS, 4, HD)
    attended = got.transpose(0, 2, 1, 3).reshape(STEPS, 4, D)
    normed, first_gap, updated = sweep_update(width, attended, start)

    rows = lax.all_to_all(normed, "z", split_axis=0, concat_axis=0, tiled=True).reshape(32, D)
    groups = gather_short(rows)
    done = [project(group, other_weight, 16 * MIB) for group in groups[:-1]]
    attended = attend(place, done, groups[-1], other_weight, True, 20 * MIB)
    pieces = attended.reshape(STEPS, 4, 8, 4, HD).transpose(0, 2, 1, 3, 4)
    got = over_all(pieces.reshape(256, 4, HD)).reshape(8, STEPS, 4, 4, HD)
    attended = got.transpose(1, 3, 0, 2, 4).reshape(STEPS, 4, D)
    pieces, marks = last_update(width, place, attended, updated, first_gap)
    totals = jnp.sum(over_all(marks), axis=0)[:, 0]
    residuals = jnp.sqrt(totals / (STEPS * TOKENS * D))
    return (deliver(place, pieces)[None], residuals)


def solution(mesh):
    fine = Mesh(mesh.devices.reshape(4, 2, 8, 4), ALL)
    placed = (P(), P(STEP, SEQ, None), P(None, None, SEQ))
    return jax.shard_map(
        local, mesh=fine, in_specs=placed, out_specs=(P(STEP, SEQ, None), P()), check_vma=False
    )
```

```python
import functools
import math

import jax
import jax.numpy as jnp
from jax import lax
from jax.experimental import pallas as pl
from jax.experimental.pallas import tpu as pltpu
from jax.sharding import Mesh, PartitionSpec as P

HD = 128
HEADS = 32
D = HEADS * HD
STEPS = 8
TOKENS = 1024
SIZES = {"x": 4, "c": 2, "z": 8, "y": 4}
STEP = ("x", "c")
SEQ = ("z", "y")
ALL = STEP + SEQ
HALF = 16
MIB = 1024 * 1024


def shift(x, axis, by):
    n = SIZES[axis]
    pairs = []
    for i in range(n):
        if axis == "x":
            pairs += [(2 * i, 2 * ((i + by) % n)), (2 * i + 1, 2 * ((i - by) % n) + 1)]
        else:
            pairs += [(i, (i + by) % n), (n + i, n + (i - by) % n)]
    return lax.ppermute(x, ("x", "c") if axis == "x" else ("c", axis), pairs)


def swap(x):
    return lax.ppermute(x, "c", [(0, 1), (1, 0)])


def join_kernel(ranges, *refs):
    *blocks, out_ref = refs
    start = 0
    for block, (low, high) in zip(blocks, ranges):
        out_ref[start : start + high - low, :] = block[low:high, :]
        start += high - low


def join(blocks, ranges=None):
    ranges = ranges or [(0, b.shape[0]) for b in blocks]
    rows = sum(high - low for low, high in ranges)
    return pl.pallas_call(
        functools.partial(join_kernel, ranges),
        out_shape=jax.ShapeDtypeStruct((rows, D), jnp.bfloat16),
        in_specs=[pl.BlockSpec(memory_space=pltpu.VMEM)] * len(blocks),
        out_specs=pl.BlockSpec(memory_space=pltpu.VMEM),
        compiler_params=pltpu.CompilerParams(vmem_limit_bytes=8 * MIB),
        cost_estimate=pl.CostEstimate(flops=0, bytes_accessed=4 * rows * D, transcendentals=0),
    )(*blocks)


SMALL_4 = (0, -1, 1, -2)
SMALL_Z = (0, -4, -1, -5, 1, -3, 2, -2)


def small_4(x, axis):
    return join([x, shift(x, axis, 1), shift(x, axis, -1), shift(x, axis, 2)])


def tie(*values):
    return lax.optimization_barrier(values)


def both_ways(up, down, axis):
    return tie(shift(up, axis, 1), shift(down, axis, -1))


def ring_of_4(x, axis):
    up, down = both_ways(x, x, axis)
    return {0: x, -1: up, 1: down, -2: shift(up, axis, 1)}


LONG = (
    ((0, -1, 1), (0,)),
    ((-2, 2), (-1, 1)),
    ((-3, 3), (-2,)),
)


def small_long(first, second, whole):
    near = [shift(first, "y", 1), shift(first, "y", -1), shift(first, "y", 2)]
    far, *near = tie(shift(whole, "z", 4), *near)
    pair = join([second, far], [(0, HALF), (HALF, 2 * HALF)])
    others = [shift(pair, "z", 1), shift(pair, "z", -1), shift(pair, "z", -2)]
    near_z = join([pair, *others, far], [(0, 2 * HALF)] * 4 + [(0, HALF)])
    return join([first, *near]), near_z


def gather_long(halves, window, weights):
    near_y, near_z = small_long(*halves)
    by_z = {0: near_y}
    up, down = both_ways(near_y, near_y, "z")
    window = over_step(window.reshape(STEPS, 4, D))
    up, down, window, *weights = tie(up, down, window, *weights)
    by_z[-1], by_z[1] = up, down
    by_z[-2], by_z[2] = both_ways(up, down, "z")
    up, down = both_ways(near_z, near_z, "y")
    by_y = {0: near_z, -1: up, 1: down}
    by_z[-2], up = tie(by_z[-2], up)
    by_y[-2] = shift(up, "y", 1)
    by_z[-3], by_z[3] = both_ways(by_z[-2], by_z[2], "z")
    groups = [[by_z[d] for d in zs] + [by_y[d] for d in ys] for zs, ys in LONG]
    return groups, window, weights


def places_long():
    places = []
    for far_z, far_y in LONG:
        places += [(dz, dy, 0, 0) for dz in far_z for dy in SMALL_4]
        for dy in far_y:
            places += [(dz, dy, 1, 0) for dz in SMALL_Z] + [(-4, dy, 0, 0)]
    return places


NEAR, FAR = (0, -1, 1), (-2,)


def gather_short(x, weight):
    near_y, near_x = tie(small_4(x[:HALF], "y"), small_4(x[HALF:], "x"))
    up, down, weight = tie(*both_ways(near_y, near_y, "x"), weight)
    by_x = {0: near_y, -1: up, 1: down, -2: shift(up, "x", 1)}
    by_y = ring_of_4(near_x, "y")
    near = [by_x[d] for d in NEAR] + [by_y[d] for d in NEAR]
    far = [by_x[d] for d in FAR] + [by_y[d] for d in FAR]
    return [near, [swap(b) for b in near], far + [swap(b) for b in far]], weight


def places_short():
    places = []
    for far in (NEAR, FAR):
        for core in (0, 1):
            places += [(dx, dy, 0, core) for dx in far for dy in SMALL_4]
            places += [(dx, dy, 1, core) for dy in far for dx in SMALL_4]
    return places


def project_rows(blocks, weight_ref, rows_ref, sems):
    copies = []
    start = 0
    for n, block in enumerate(blocks):
        rows = block.shape[0]
        copies.append(
            pltpu.make_async_copy(block, rows_ref.at[pl.ds(start, rows), :], sems.at[n])
        )
        copies[-1].start()
        start += rows
    for copy in copies:
        copy.wait()
    out = jnp.dot(rows_ref[...], weight_ref[...], preferred_element_type=jnp.float32)
    return out.astype(jnp.bfloat16)


def project_kernel(*refs):
    *blocks, weight_ref, out_ref, rows_ref, sems = refs
    out_ref[...] = project_rows(blocks, weight_ref, rows_ref, sems)


def project(blocks, weight, limit):
    rows = sum(b.shape[0] for b in blocks)
    vmem = pl.BlockSpec(memory_space=pltpu.VMEM)
    return pl.pallas_call(
        project_kernel,
        out_shape=jax.ShapeDtypeStruct((rows, 3 * HD), jnp.bfloat16),
        in_specs=[pl.BlockSpec(memory_space=pl.ANY)] * len(blocks) + [vmem],
        out_specs=vmem,
        scratch_shapes=[
            pltpu.VMEM((rows, D), jnp.bfloat16),
            pltpu.SemaphoreType.DMA((len(blocks),)),
        ],
        compiler_params=pltpu.CompilerParams(vmem_limit_bytes=limit),
        cost_estimate=pl.CostEstimate(
            flops=6 * rows * D * HD, bytes_accessed=2 * rows * D, transcendentals=0
        ),
    )(*blocks, weight)


def attend_kernel(short, ready, place, *refs):
    *blocks, weight_ref, out_ref, rows_ref, qkv_ref, sems = refs
    blocks, done = blocks[ready:], blocks[:ready]
    start = 0
    for part in done:
        qkv_ref[start : start + part.shape[0], :] = part[...]
        start += part.shape[0]
    qkv_ref[start:, :] = project_rows(blocks, weight_ref, rows_ref, sems)
    factor = math.log2(math.e) / math.sqrt(HD)
    x, core, z, y = place[0], place[1], place[2], place[3]
    keys = qkv_ref[:, HD : 2 * HD]
    values = qkv_ref[:, 2 * HD :]
    places = places_short() if short else places_long()
    size = 256
    for b in range(TOKENS // size):
        query = qkv_ref[b * size : (b + 1) * size, :HD]
        scores = lax.dot_general(
            query, keys, (((1,), (1,)), ((), ())), preferred_element_type=jnp.float32
        )
        peak = jnp.max(scores, axis=-1, keepdims=True)
        expo = jnp.exp2((scores - peak) * factor)
        total = jnp.sum(expo, axis=-1, keepdims=True)
        mixed = jnp.dot(expo.astype(jnp.bfloat16), values, preferred_element_type=jnp.float32)
        mixed = (mixed / total).astype(jnp.bfloat16)
        for r in range(size // HALF):
            far, dy, half, other = places[b * (size // HALF) + r]
            owner = 1 - core if other else core
            sign = 1 - 2 * owner
            row = lax.rem(y + sign * dy + 4, 4)
            if short:
                slot = (2 * lax.rem(x + sign * far + 4, 4) + owner) * 4 + row
            else:
                slot = lax.rem(z + sign * far + 8, 8) * 4 + row
            out_ref[slot, half * HALF : (half + 1) * HALF, :] = mixed[r * HALF : (r + 1) * HALF]


def attend(place, done, blocks, weight, short, limit):
    rows = sum(b.shape[0] for b in blocks)
    vmem = pl.BlockSpec(memory_space=pltpu.VMEM)
    return pl.pallas_call(
        functools.partial(attend_kernel, short, len(done)),
        out_shape=jax.ShapeDtypeStruct((TOKENS // 32, 32, HD), jnp.bfloat16),
        in_specs=[pl.BlockSpec(memory_space=pltpu.SMEM)]
        + [vmem] * len(done)
        + [pl.BlockSpec(memory_space=pl.ANY)] * len(blocks)
        + [vmem],
        out_specs=vmem,
        scratch_shapes=[
            pltpu.VMEM((rows, D), jnp.bfloat16),
            pltpu.VMEM((TOKENS, 3 * HD), jnp.bfloat16),
            pltpu.SemaphoreType.DMA((len(blocks),)),
        ],
        compiler_params=pltpu.CompilerParams(vmem_limit_bytes=limit),
        cost_estimate=pl.CostEstimate(
            flops=4 * TOKENS * TOKENS * HD + 6 * rows * D * HD,
            bytes_accessed=2 * rows * D,
            transcendentals=TOKENS * TOKENS,
        ),
    )(place, *done, *blocks, weight)


def weight_kernel(place, weight_ref, out_ref, masked_ref):
    wanted = 2 * place[0] + place[1] == place[2]
    for c in range(3):
        part = weight_ref[c]
        out_ref[:, c * HD : (c + 1) * HD] = part
        masked_ref[:, c * HD : (c + 1) * HD] = jnp.where(wanted, part, jnp.zeros_like(part))


def side_by_side(place, weight):
    out = jax.ShapeDtypeStruct((D, 3 * HD), jnp.bfloat16)
    vmem = pl.BlockSpec(memory_space=pltpu.VMEM)
    return pl.pallas_call(
        weight_kernel,
        out_shape=[out, out],
        in_specs=[pl.BlockSpec(memory_space=pltpu.SMEM), vmem],
        out_specs=[vmem, vmem],
        compiler_params=pltpu.CompilerParams(vmem_limit_bytes=16 * MIB),
        cost_estimate=pl.CostEstimate(flops=0, bytes_accessed=18 * D * HD, transcendentals=0),
    )(place, weight)


def norm(values):
    center = jnp.mean(values, axis=-1, keepdims=True)
    moved = values - center
    spread = jnp.mean(moved * moved, axis=-1, keepdims=True)
    return moved * lax.rsqrt(spread + 1e-05)


def norm_kernel(rows_ref, first_ref, second_ref, whole_ref):
    for n, out_ref in enumerate((first_ref, second_ref)):
        half = norm(rows_ref[n * HALF : (n + 1) * HALF, :]).astype(jnp.bfloat16)
        out_ref[...] = half
        whole_ref[n * HALF : (n + 1) * HALF, :] = half


def layer_norm(rows):
    half = jax.ShapeDtypeStruct((HALF, D), jnp.bfloat16)
    whole = jax.ShapeDtypeStruct((2 * HALF, D), jnp.bfloat16)
    return pl.pallas_call(
        norm_kernel,
        out_shape=[half, half, whole],
        compiler_params=pltpu.CompilerParams(vmem_limit_bytes=8 * MIB),
    )(rows)


def sweep_steps(width, attended_ref, current_ref, store):
    anchor = current_ref[0]
    before = jnp.zeros_like(anchor)
    gap = jnp.zeros_like(anchor)
    for k in range(STEPS):
        current = current_ref[k]
        increment = width[k] * (attended_ref[k].astype(jnp.float32) - current)
        updated = anchor + before
        change = updated - current
        gap = gap + change * change
        store(k, updated, increment)
        before = before + increment
    return jnp.sum(gap)


def sweep_kernel(width, attended_ref, current_ref, normed_ref, gap_ref, updated_ref):
    def store(k, updated, increment):
        updated_ref[k] = updated
        normed_ref[k] = norm(updated).astype(jnp.bfloat16)

    gap = sweep_steps(width, attended_ref, current_ref, store)
    gap_ref[...] = jnp.broadcast_to(gap, gap_ref.shape)


def sweep_update(width, attended, current):
    shape = current.shape
    vmem = pl.BlockSpec(memory_space=pltpu.VMEM)
    return pl.pallas_call(
        sweep_kernel,
        out_shape=[
            jax.ShapeDtypeStruct(shape, jnp.bfloat16),
            jax.ShapeDtypeStruct((1, 1, 128), jnp.float32),
            jax.ShapeDtypeStruct(shape, jnp.float32),
        ],
        in_specs=[pl.BlockSpec(memory_space=pltpu.SMEM)] + [vmem] * 2,
        out_specs=[vmem] * 3,
    )(width, attended, current)


def step_pair(place, far, flip):
    return 2 * lax.rem(place[0] + far, 4) + lax.rem(place[1] + flip, 2)


def last_kernel(width, place, attended_ref, current_ref, first_ref, *refs):
    *piece_refs, marks_ref, advanced_ref = refs

    def store(k, updated, increment):
        advanced_ref[k] = updated + increment

    gap = sweep_steps(width, attended_ref, current_ref, store)
    for n, piece_ref in enumerate(piece_refs):
        piece_ref[...] = advanced_ref[step_pair(place, n // 2, n % 2)]
    marks_ref[:, 0:1, :] = jnp.broadcast_to(first_ref[...], (256, 1, 128))
    marks_ref[:, 1:2, :] = jnp.broadcast_to(gap, (256, 1, 128))


def last_update(width, place, attended, current, first_gap):
    vmem = pl.BlockSpec(memory_space=pltpu.VMEM)
    smem = pl.BlockSpec(memory_space=pltpu.SMEM)
    *pieces, marks = pl.pallas_call(
        last_kernel,
        out_shape=[jax.ShapeDtypeStruct(current.shape[1:], jnp.float32)] * STEPS
        + [jax.ShapeDtypeStruct((256, 2, 128), jnp.float32)],
        in_specs=[smem, smem] + [vmem] * 3,
        out_specs=[vmem] * (STEPS + 1),
        scratch_shapes=[pltpu.VMEM(current.shape, jnp.float32)],
    )(width, place, attended, current, first_gap)
    return pieces, marks


def over_step(pieces):
    return lax.all_to_all(pieces, STEP, split_axis=0, concat_axis=0, tiled=True)


def over_all(pieces):
    return lax.all_to_all(pieces, ALL, split_axis=0, concat_axis=0, tiled=True)


def deliver_kernel(place, *refs):
    *pieces, out_ref = refs
    swapped = place[1] == 1
    for far in range(4):
        same, other = pieces[2 * far][...], pieces[2 * far + 1][...]
        low = jnp.where(swapped, other, same)
        high = jnp.where(swapped, same, other)
        x = lax.rem(place[0] - far + 4, 4)
        out_ref[pl.ds(pl.multiple_of(8 * x, 8), 8), :] = jnp.concatenate([low, high], axis=0)


def deliver(place, pieces):
    got = pieces[:1]
    for n in range(1, STEPS):
        pairs = [
            (2 * i + c, 2 * ((i + n // 2) % 4) + (c + n) % 2) for i in range(4) for c in range(2)
        ]
        got.append(lax.ppermute(pieces[n], STEP, pairs))
    vmem = pl.BlockSpec(memory_space=pltpu.VMEM)
    return pl.pallas_call(
        deliver_kernel,
        out_shape=jax.ShapeDtypeStruct((32, D), jnp.float32),
        in_specs=[pl.BlockSpec(memory_space=pltpu.SMEM)] + [vmem] * STEPS,
        out_specs=vmem,
    )(place, *got)


def local(step_index, window_init, qkv_weight):
    window = window_init[0]
    place = jnp.stack([lax.axis_index(a) for a in ALL]).astype(jnp.int32)
    width = (step_index[:-1] - step_index[1:]).astype(jnp.float32) / 1000.0
    weights = side_by_side(place, qkv_weight)
    groups, start, (weight, masked) = gather_long(layer_norm(window), window, weights)
    other_weight = lax.psum(masked, "z")
    done = [project(group, weight, 24 * MIB) for group in groups[:-1]]
    attended = attend(place, done, groups[-1], weight, False, 24 * MIB)
    pieces = attended.reshape(32, STEPS, 4, HD).transpose(1, 0, 2, 3)
    got = over_all(pieces.reshape(256, 4, HD)).reshape(STEPS, HEADS, 4, HD)
    attended = got.transpose(0, 2, 1, 3).reshape(STEPS, 4, D)
    normed, first_gap, updated = sweep_update(width, attended, start)

    rows = lax.all_to_all(normed, "z", split_axis=0, concat_axis=0, tiled=True).reshape(32, D)
    groups, other_weight = gather_short(rows, other_weight)
    done = [project(group, other_weight, 16 * MIB) for group in groups[:-1]]
    attended = attend(place, done, groups[-1], other_weight, True, 20 * MIB)
    pieces = attended.reshape(STEPS, 4, 8, 4, HD).transpose(0, 2, 1, 3, 4)
    got = over_all(pieces.reshape(256, 4, HD)).reshape(8, STEPS, 4, 4, HD)
    attended = got.transpose(1, 3, 0, 2, 4).reshape(STEPS, 4, D)
    pieces, marks = last_update(width, place, attended, updated, first_gap)
    totals = jnp.sum(over_all(marks), axis=0)[:, 0]
    residuals = jnp.sqrt(totals / (STEPS * TOKENS * D))
    return (deliver(place, pieces)[None], residuals)


def solution(mesh):
    fine = Mesh(mesh.devices.reshape(4, 2, 8, 4), ALL)
    placed = (P(), P(STEP, SEQ, None), P(None, None, SEQ))
    return jax.shard_map(
        local, mesh=fine, in_specs=placed, out_specs=(P(STEP, SEQ, None), P()), check_vma=False
    )
```

```python
import functools
import math

import jax
import jax.numpy as jnp
from jax import lax
from jax.experimental import pallas as pl
from jax.experimental.pallas import tpu as pltpu
from jax.sharding import Mesh, PartitionSpec as P

HD = 128
HEADS = 32
D = HEADS * HD
STEPS = 8
TOKENS = 1024
SIZES = {"x": 4, "c": 2, "z": 8, "y": 4}
STEP = ("x", "c")
SEQ = ("z", "y")
ALL = STEP + SEQ
HALF = 16
MIB = 1024 * 1024


def shift(x, axis, by):
    n = SIZES[axis]
    pairs = []
    for i in range(n):
        if axis == "x":
            pairs += [(2 * i, 2 * ((i + by) % n)), (2 * i + 1, 2 * ((i - by) % n) + 1)]
        else:
            pairs += [(i, (i + by) % n), (n + i, n + (i - by) % n)]
    return lax.ppermute(x, ("x", "c") if axis == "x" else ("c", axis), pairs)


def swap(x):
    return lax.ppermute(x, "c", [(0, 1), (1, 0)])


def join_kernel(ranges, *refs):
    *blocks, out_ref = refs
    start = 0
    for block, (low, high) in zip(blocks, ranges):
        out_ref[start : start + high - low, :] = block[low:high, :]
        start += high - low


def join(blocks, ranges=None):
    ranges = ranges or [(0, b.shape[0]) for b in blocks]
    rows = sum(high - low for low, high in ranges)
    return pl.pallas_call(
        functools.partial(join_kernel, ranges),
        out_shape=jax.ShapeDtypeStruct((rows, D), jnp.bfloat16),
        in_specs=[pl.BlockSpec(memory_space=pltpu.VMEM)] * len(blocks),
        out_specs=pl.BlockSpec(memory_space=pltpu.VMEM),
        compiler_params=pltpu.CompilerParams(vmem_limit_bytes=8 * MIB),
        cost_estimate=pl.CostEstimate(flops=0, bytes_accessed=4 * rows * D, transcendentals=0),
    )(*blocks)


SMALL_4 = (0, -1, 1, -2)
SMALL_Z = (0, -4, -1, -5, 1, -3, 2, -2)


def small_4(x, axis):
    return join([x, shift(x, axis, 1), shift(x, axis, -1), shift(x, axis, 2)])


def tie(*values):
    return lax.optimization_barrier(values)


def both_ways(up, down, axis):
    return tie(shift(up, axis, 1), shift(down, axis, -1))


def ring_of_4(x, axis):
    up, down = both_ways(x, x, axis)
    return {0: x, -1: up, 1: down, -2: shift(up, axis, 1)}


LONG = (
    ((0, -1, 1), (0,)),
    ((-2, 2), (-1, 1)),
    ((-3, 3), (-2,)),
)


def small_long(first, second, whole):
    near = [shift(first, "y", 1), shift(first, "y", -1), shift(first, "y", 2)]
    far, *near = tie(shift(whole, "z", 4), *near)
    pair = join([second, far], [(0, HALF), (HALF, 2 * HALF)])
    near_y, pair = tie(join([first, *near]), pair)
    others = [shift(pair, "z", 1), shift(pair, "z", -1), shift(pair, "z", -2)]
    near_z = join([pair, *others, far], [(0, 2 * HALF)] * 4 + [(0, HALF)])
    return near_y, near_z


def gather_long(halves, window, weights):
    near_y, near_z = small_long(*halves)
    by_z = {0: near_y}
    up, down = both_ways(near_y, near_y, "z")
    up, near_z = tie(up, near_z)
    window = over_step(window.reshape(STEPS, 4, D))
    up, down, window, *weights = tie(up, down, window, *weights)
    by_z[-1], by_z[1] = up, down
    by_z[-2], by_z[2] = both_ways(up, down, "z")
    up, down = both_ways(near_z, near_z, "y")
    by_y = {0: near_z, -1: up, 1: down}
    by_z[-2], up = tie(by_z[-2], up)
    by_y[-2] = shift(up, "y", 1)
    by_z[-3], by_z[3] = both_ways(by_z[-2], by_z[2], "z")
    groups = [[by_z[d] for d in zs] + [by_y[d] for d in ys] for zs, ys in LONG]
    return groups, window, weights


def places_long():
    places = []
    for far_z, far_y in LONG:
        places += [(dz, dy, 0, 0) for dz in far_z for dy in SMALL_4]
        for dy in far_y:
            places += [(dz, dy, 1, 0) for dz in SMALL_Z] + [(-4, dy, 0, 0)]
    return places


NEAR, FAR = (0, -1, 1), (-2,)


def project_short(x, weight):
    near_y, near_x = tie(small_4(x[:HALF], "y"), small_4(x[HALF:], "x"))
    up, down, weight = tie(*both_ways(near_y, near_y, "x"), weight)
    by_x = {0: near_y, -1: up, 1: down, -2: shift(up, "x", 1)}
    by_y = ring_of_4(near_x, "y")
    near = [by_x[d] for d in NEAR] + [by_y[d] for d in NEAR]
    done = [project(blocks, weight, 16 * MIB) for blocks in (near, [swap(b) for b in near])]
    far = [by_x[d] for d in FAR] + [by_y[d] for d in FAR]
    *far, first, second = tie(*far, *done)
    return [first, second], far + [swap(b) for b in far], weight


def places_short():
    places = []
    for far in (NEAR, FAR):
        for core in (0, 1):
            places += [(dx, dy, 0, core) for dx in far for dy in SMALL_4]
            places += [(dx, dy, 1, core) for dy in far for dx in SMALL_4]
    return places


def project_rows(blocks, weight_ref, rows_ref, sems):
    copies = []
    start = 0
    for n, block in enumerate(blocks):
        rows = block.shape[0]
        copies.append(
            pltpu.make_async_copy(block, rows_ref.at[pl.ds(start, rows), :], sems.at[n])
        )
        copies[-1].start()
        start += rows
    for copy in copies:
        copy.wait()
    out = jnp.dot(rows_ref[...], weight_ref[...], preferred_element_type=jnp.float32)
    return out.astype(jnp.bfloat16)


def project_kernel(*refs):
    *blocks, weight_ref, out_ref, rows_ref, sems = refs
    out_ref[...] = project_rows(blocks, weight_ref, rows_ref, sems)


def project(blocks, weight, limit):
    rows = sum(b.shape[0] for b in blocks)
    vmem = pl.BlockSpec(memory_space=pltpu.VMEM)
    return pl.pallas_call(
        project_kernel,
        out_shape=jax.ShapeDtypeStruct((rows, 3 * HD), jnp.bfloat16),
        in_specs=[pl.BlockSpec(memory_space=pl.ANY)] * len(blocks) + [vmem],
        out_specs=vmem,
        scratch_shapes=[
            pltpu.VMEM((rows, D), jnp.bfloat16),
            pltpu.SemaphoreType.DMA((len(blocks),)),
        ],
        compiler_params=pltpu.CompilerParams(vmem_limit_bytes=limit),
        cost_estimate=pl.CostEstimate(
            flops=6 * rows * D * HD, bytes_accessed=2 * rows * D, transcendentals=0
        ),
    )(*blocks, weight)


def attend_kernel(short, ready, place, *refs):
    *blocks, weight_ref, out_ref, rows_ref, qkv_ref, sems = refs
    blocks, done = blocks[ready:], blocks[:ready]
    start = 0
    for part in done:
        qkv_ref[start : start + part.shape[0], :] = part[...]
        start += part.shape[0]
    qkv_ref[start:, :] = project_rows(blocks, weight_ref, rows_ref, sems)
    factor = math.log2(math.e) / math.sqrt(HD)
    x, core, z, y = place[0], place[1], place[2], place[3]
    keys = qkv_ref[:, HD : 2 * HD]
    values = qkv_ref[:, 2 * HD :]
    places = places_short() if short else places_long()
    size = 256
    for b in range(TOKENS // size):
        query = qkv_ref[b * size : (b + 1) * size, :HD]
        scores = lax.dot_general(
            query, keys, (((1,), (1,)), ((), ())), preferred_element_type=jnp.float32
        )
        peak = jnp.max(scores, axis=-1, keepdims=True)
        expo = jnp.exp2((scores - peak) * factor)
        total = jnp.sum(expo, axis=-1, keepdims=True)
        mixed = jnp.dot(expo.astype(jnp.bfloat16), values, preferred_element_type=jnp.float32)
        mixed = (mixed / total).astype(jnp.bfloat16)
        for r in range(size // HALF):
            far, dy, half, other = places[b * (size // HALF) + r]
            owner = 1 - core if other else core
            sign = 1 - 2 * owner
            row = lax.rem(y + sign * dy + 4, 4)
            if short:
                slot = (2 * lax.rem(x + sign * far + 4, 4) + owner) * 4 + row
            else:
                slot = lax.rem(z + sign * far + 8, 8) * 4 + row
            out_ref[slot, half * HALF : (half + 1) * HALF, :] = mixed[r * HALF : (r + 1) * HALF]


def attend(place, done, blocks, weight, short, limit):
    rows = sum(b.shape[0] for b in blocks)
    vmem = pl.BlockSpec(memory_space=pltpu.VMEM)
    return pl.pallas_call(
        functools.partial(attend_kernel, short, len(done)),
        out_shape=jax.ShapeDtypeStruct((TOKENS // 32, 32, HD), jnp.bfloat16),
        in_specs=[pl.BlockSpec(memory_space=pltpu.SMEM)]
        + [vmem] * len(done)
        + [pl.BlockSpec(memory_space=pl.ANY)] * len(blocks)
        + [vmem],
        out_specs=vmem,
        scratch_shapes=[
            pltpu.VMEM((rows, D), jnp.bfloat16),
            pltpu.VMEM((TOKENS, 3 * HD), jnp.bfloat16),
            pltpu.SemaphoreType.DMA((len(blocks),)),
        ],
        compiler_params=pltpu.CompilerParams(vmem_limit_bytes=limit),
        cost_estimate=pl.CostEstimate(
            flops=4 * TOKENS * TOKENS * HD + 6 * rows * D * HD,
            bytes_accessed=2 * rows * D,
            transcendentals=TOKENS * TOKENS,
        ),
    )(place, *done, *blocks, weight)


def weight_kernel(place, weight_ref, out_ref, masked_ref):
    wanted = 2 * place[0] + place[1] == place[2]
    for c in range(3):
        part = weight_ref[c]
        out_ref[:, c * HD : (c + 1) * HD] = part
        masked_ref[:, c * HD : (c + 1) * HD] = jnp.where(wanted, part, jnp.zeros_like(part))


def side_by_side(place, weight):
    out = jax.ShapeDtypeStruct((D, 3 * HD), jnp.bfloat16)
    vmem = pl.BlockSpec(memory_space=pltpu.VMEM)
    return pl.pallas_call(
        weight_kernel,
        out_shape=[out, out],
        in_specs=[pl.BlockSpec(memory_space=pltpu.SMEM), vmem],
        out_specs=[vmem, vmem],
        compiler_params=pltpu.CompilerParams(vmem_limit_bytes=16 * MIB),
        cost_estimate=pl.CostEstimate(flops=0, bytes_accessed=18 * D * HD, transcendentals=0),
    )(place, weight)


def norm(values):
    center = jnp.mean(values, axis=-1, keepdims=True)
    moved = values - center
    spread = jnp.mean(moved * moved, axis=-1, keepdims=True)
    return moved * lax.rsqrt(spread + 1e-05)


def norm_kernel(rows_ref, first_ref, second_ref, whole_ref):
    for n, out_ref in enumerate((first_ref, second_ref)):
        half = norm(rows_ref[n * HALF : (n + 1) * HALF, :]).astype(jnp.bfloat16)
        out_ref[...] = half
        whole_ref[n * HALF : (n + 1) * HALF, :] = half


def layer_norm(rows):
    half = jax.ShapeDtypeStruct((HALF, D), jnp.bfloat16)
    whole = jax.ShapeDtypeStruct((2 * HALF, D), jnp.bfloat16)
    return pl.pallas_call(
        norm_kernel,
        out_shape=[half, half, whole],
        compiler_params=pltpu.CompilerParams(vmem_limit_bytes=8 * MIB),
    )(rows)


def sweep_steps(width, attended_ref, current_ref, store):
    anchor = current_ref[0]
    before = jnp.zeros_like(anchor)
    gap = jnp.zeros_like(anchor)
    for k in range(STEPS):
        current = current_ref[k]
        increment = width[k] * (attended_ref[k].astype(jnp.float32) - current)
        updated = anchor + before
        change = updated - current
        gap = gap + change * change
        store(k, updated, increment)
        before = before + increment
    return jnp.sum(gap)


def sweep_kernel(width, attended_ref, current_ref, normed_ref, gap_ref, updated_ref):
    def store(k, updated, increment):
        updated_ref[k] = updated
        normed_ref[k] = norm(updated).astype(jnp.bfloat16)

    gap = sweep_steps(width, attended_ref, current_ref, store)
    gap_ref[...] = jnp.broadcast_to(gap, gap_ref.shape)


def sweep_update(width, attended, current):
    shape = current.shape
    vmem = pl.BlockSpec(memory_space=pltpu.VMEM)
    return pl.pallas_call(
        sweep_kernel,
        out_shape=[
            jax.ShapeDtypeStruct(shape, jnp.bfloat16),
            jax.ShapeDtypeStruct((1, 1, 128), jnp.float32),
            jax.ShapeDtypeStruct(shape, jnp.float32),
        ],
        in_specs=[pl.BlockSpec(memory_space=pltpu.SMEM)] + [vmem] * 2,
        out_specs=[vmem] * 3,
    )(width, attended, current)


def step_pair(place, far, flip):
    return 2 * lax.rem(place[0] + far, 4) + lax.rem(place[1] + flip, 2)


def last_kernel(width, place, attended_ref, current_ref, first_ref, *refs):
    *piece_refs, marks_ref, advanced_ref = refs

    def store(k, updated, increment):
        advanced_ref[k] = updated + increment

    gap = sweep_steps(width, attended_ref, current_ref, store)
    for n, piece_ref in enumerate(piece_refs):
        piece_ref[...] = advanced_ref[step_pair(place, n // 2, n % 2)]
    marks_ref[:, 0:1, :] = jnp.broadcast_to(first_ref[...], (256, 1, 128))
    marks_ref[:, 1:2, :] = jnp.broadcast_to(gap, (256, 1, 128))


def last_update(width, place, attended, current, first_gap):
    vmem = pl.BlockSpec(memory_space=pltpu.VMEM)
    smem = pl.BlockSpec(memory_space=pltpu.SMEM)
    *pieces, marks = pl.pallas_call(
        last_kernel,
        out_shape=[jax.ShapeDtypeStruct(current.shape[1:], jnp.float32)] * STEPS
        + [jax.ShapeDtypeStruct((256, 2, 128), jnp.float32)],
        in_specs=[smem, smem] + [vmem] * 3,
        out_specs=[vmem] * (STEPS + 1),
        scratch_shapes=[pltpu.VMEM(current.shape, jnp.float32)],
    )(width, place, attended, current, first_gap)
    return pieces, marks


def over_step(pieces):
    return lax.all_to_all(pieces, STEP, split_axis=0, concat_axis=0, tiled=True)


def over_all(pieces):
    return lax.all_to_all(pieces, ALL, split_axis=0, concat_axis=0, tiled=True)


def deliver_kernel(place, *refs):
    *pieces, out_ref = refs
    swapped = place[1] == 1
    for far in range(4):
        same, other = pieces[2 * far][...], pieces[2 * far + 1][...]
        low = jnp.where(swapped, other, same)
        high = jnp.where(swapped, same, other)
        x = lax.rem(place[0] - far + 4, 4)
        out_ref[pl.ds(pl.multiple_of(8 * x, 8), 8), :] = jnp.concatenate([low, high], axis=0)


def deliver(place, pieces):
    got = pieces[:1]
    for n in range(1, STEPS):
        pairs = [
            (2 * i + c, 2 * ((i + n // 2) % 4) + (c + n) % 2) for i in range(4) for c in range(2)
        ]
        got.append(lax.ppermute(pieces[n], STEP, pairs))
    vmem = pl.BlockSpec(memory_space=pltpu.VMEM)
    return pl.pallas_call(
        deliver_kernel,
        out_shape=jax.ShapeDtypeStruct((32, D), jnp.float32),
        in_specs=[pl.BlockSpec(memory_space=pltpu.SMEM)] + [vmem] * STEPS,
        out_specs=vmem,
    )(place, *got)


def local(step_index, window_init, qkv_weight):
    window = window_init[0]
    place = jnp.stack([lax.axis_index(a) for a in ALL]).astype(jnp.int32)
    width = (step_index[:-1] - step_index[1:]).astype(jnp.float32) / 1000.0
    weights = side_by_side(place, qkv_weight)
    groups, start, (weight, masked) = gather_long(layer_norm(window), window, weights)
    other_weight = lax.psum(masked, "z")
    done = [project(group, weight, 24 * MIB) for group in groups[:-1]]
    attended = attend(place, done, groups[-1], weight, False, 24 * MIB)
    pieces = attended.reshape(32, STEPS, 4, HD).transpose(1, 0, 2, 3)
    got = over_all(pieces.reshape(256, 4, HD)).reshape(STEPS, HEADS, 4, HD)
    attended = got.transpose(0, 2, 1, 3).reshape(STEPS, 4, D)
    normed, first_gap, updated = sweep_update(width, attended, start)

    rows = lax.all_to_all(normed, "z", split_axis=0, concat_axis=0, tiled=True).reshape(32, D)
    done, blocks, other_weight = project_short(rows, other_weight)
    attended = attend(place, done, blocks, other_weight, True, 20 * MIB)
    pieces = attended.reshape(STEPS, 4, 8, 4, HD).transpose(0, 2, 1, 3, 4)
    got = over_all(pieces.reshape(256, 4, HD)).reshape(8, STEPS, 4, 4, HD)
    attended = got.transpose(1, 3, 0, 2, 4).reshape(STEPS, 4, D)
    pieces, marks = last_update(width, place, attended, updated, first_gap)
    totals = jnp.sum(over_all(marks), axis=0)[:, 0]
    residuals = jnp.sqrt(totals / (STEPS * TOKENS * D))
    return (deliver(place, pieces)[None], residuals)


def solution(mesh):
    fine = Mesh(mesh.devices.reshape(4, 2, 8, 4), ALL)
    placed = (P(), P(STEP, SEQ, None), P(None, None, SEQ))
    return jax.shard_map(
        local, mesh=fine, in_specs=placed, out_specs=(P(STEP, SEQ, None), P()), check_vma=False
    )
```

```python
import functools
import math

import jax
import jax.numpy as jnp
from jax import lax
from jax.experimental import pallas as pl
from jax.experimental.pallas import tpu as pltpu
from jax.sharding import Mesh, PartitionSpec as P

HD = 128
HEADS = 32
D = HEADS * HD
STEPS = 8
TOKENS = 1024
SIZES = {"x": 4, "c": 2, "z": 8, "y": 4}
STEP = ("x", "c")
SEQ = ("z", "y")
ALL = STEP + SEQ
HALF = 16
MIB = 1024 * 1024


def shift(x, axis, by):
    n = SIZES[axis]
    pairs = []
    for i in range(n):
        if axis == "x":
            pairs += [(2 * i, 2 * ((i + by) % n)), (2 * i + 1, 2 * ((i - by) % n) + 1)]
        else:
            pairs += [(i, (i + by) % n), (n + i, n + (i - by) % n)]
    return lax.ppermute(x, ("x", "c") if axis == "x" else ("c", axis), pairs)


def swap(x):
    return lax.ppermute(x, "c", [(0, 1), (1, 0)])


def join_kernel(ranges, *refs):
    *blocks, out_ref = refs
    start = 0
    for block, (low, high) in zip(blocks, ranges):
        out_ref[start : start + high - low, :] = block[low:high, :]
        start += high - low


def join(blocks, ranges=None):
    ranges = ranges or [(0, b.shape[0]) for b in blocks]
    rows = sum(high - low for low, high in ranges)
    return pl.pallas_call(
        functools.partial(join_kernel, ranges),
        out_shape=jax.ShapeDtypeStruct((rows, D), jnp.bfloat16),
        in_specs=[pl.BlockSpec(memory_space=pltpu.VMEM)] * len(blocks),
        out_specs=pl.BlockSpec(memory_space=pltpu.VMEM),
        compiler_params=pltpu.CompilerParams(vmem_limit_bytes=8 * MIB),
        cost_estimate=pl.CostEstimate(flops=0, bytes_accessed=4 * rows * D, transcendentals=0),
    )(*blocks)


SMALL_4 = (0, -1, 1, -2)
SMALL_Z = (0, -4, -1, -5, 1, -3, 2, -2)


def small_4(x, axis):
    return join([x, shift(x, axis, 1), shift(x, axis, -1), shift(x, axis, 2)])


def tie(*values):
    return lax.optimization_barrier(values)


def both_ways(up, down, axis):
    return tie(shift(up, axis, 1), shift(down, axis, -1))


def ring_of_4(x, axis):
    up, down = both_ways(x, x, axis)
    return {0: x, -1: up, 1: down, -2: shift(up, axis, 1)}


LONG = (
    ((0, -1, 1), (0,)),
    ((-2, 2), (-1, 1)),
    ((-3, 3), (-2,)),
)


def small_long(first, second, whole):
    near = [shift(first, "y", 1), shift(first, "y", -1), shift(first, "y", 2)]
    far, *near = tie(shift(whole, "z", 4), *near)
    pair = join([second, far], [(0, HALF), (HALF, 2 * HALF)])
    near_y, pair = tie(join([first, *near]), pair)
    others = [shift(pair, "z", 1), shift(pair, "z", -1), shift(pair, "z", -2)]
    near_z = join([pair, *others, far], [(0, 2 * HALF)] * 4 + [(0, HALF)])
    return near_y, near_z


def gather_long(halves, window, weights):
    near_y, near_z = small_long(*halves)
    by_z = {0: near_y}
    up, down = both_ways(near_y, near_y, "z")
    window = over_step(window.reshape(STEPS, 4, D))
    by_z[-1], by_z[1] = up, down
    up, down, window, *weights = tie(*both_ways(up, down, "z"), window, *weights)
    by_z[-2], by_z[2] = up, down
    by_z[-3], by_z[3] = both_ways(up, down, "z")
    up, down = both_ways(near_z, near_z, "y")
    by_y = {0: near_z, -1: up, 1: down}
    by_z[-2], up = tie(by_z[-2], up)
    by_y[-2] = shift(up, "y", 1)
    groups = [[by_z[d] for d in zs] + [by_y[d] for d in ys] for zs, ys in LONG]
    return groups, window, weights


def places_long():
    places = []
    for far_z, far_y in LONG:
        places += [(dz, dy, 0, 0) for dz in far_z for dy in SMALL_4]
        for dy in far_y:
            places += [(dz, dy, 1, 0) for dz in SMALL_Z] + [(-4, dy, 0, 0)]
    return places


NEAR, FAR = (0, -1, 1), (-2,)


def project_short(x, weight):
    near_y, near_x = tie(small_4(x[:HALF], "y"), small_4(x[HALF:], "x"))
    up, down, weight = tie(*both_ways(near_y, near_y, "x"), weight)
    by_x = {0: near_y, -1: up, 1: down, -2: shift(up, "x", 1)}
    by_y = ring_of_4(near_x, "y")
    near = [by_x[d] for d in NEAR] + [by_y[d] for d in NEAR]
    done = [project(blocks, weight, 16 * MIB) for blocks in (near, [swap(b) for b in near])]
    far = [by_x[d] for d in FAR] + [by_y[d] for d in FAR]
    *far, first, second = tie(*far, *done)
    return [first, second], far + [swap(b) for b in far], weight


def places_short():
    places = []
    for far in (NEAR, FAR):
        for core in (0, 1):
            places += [(dx, dy, 0, core) for dx in far for dy in SMALL_4]
            places += [(dx, dy, 1, core) for dy in far for dx in SMALL_4]
    return places


def project_rows(blocks, weight_ref, rows_ref, sems):
    copies = []
    start = 0
    for n, block in enumerate(blocks):
        rows = block.shape[0]
        copies.append(
            pltpu.make_async_copy(block, rows_ref.at[pl.ds(start, rows), :], sems.at[n])
        )
        copies[-1].start()
        start += rows
    for copy in copies:
        copy.wait()
    out = jnp.dot(rows_ref[...], weight_ref[...], preferred_element_type=jnp.float32)
    return out.astype(jnp.bfloat16)


def project_kernel(*refs):
    *blocks, weight_ref, out_ref, rows_ref, sems = refs
    out_ref[...] = project_rows(blocks, weight_ref, rows_ref, sems)


def project(blocks, weight, limit):
    rows = sum(b.shape[0] for b in blocks)
    vmem = pl.BlockSpec(memory_space=pltpu.VMEM)
    return pl.pallas_call(
        project_kernel,
        out_shape=jax.ShapeDtypeStruct((rows, 3 * HD), jnp.bfloat16),
        in_specs=[pl.BlockSpec(memory_space=pl.ANY)] * len(blocks) + [vmem],
        out_specs=vmem,
        scratch_shapes=[
            pltpu.VMEM((rows, D), jnp.bfloat16),
            pltpu.SemaphoreType.DMA((len(blocks),)),
        ],
        compiler_params=pltpu.CompilerParams(vmem_limit_bytes=limit),
        cost_estimate=pl.CostEstimate(
            flops=6 * rows * D * HD, bytes_accessed=2 * rows * D, transcendentals=0
        ),
    )(*blocks, weight)


def attend_kernel(short, ready, place, *refs):
    *blocks, weight_ref, out_ref, rows_ref, qkv_ref, sems = refs
    blocks, done = blocks[ready:], blocks[:ready]
    start = 0
    for part in done:
        qkv_ref[start : start + part.shape[0], :] = part[...]
        start += part.shape[0]
    qkv_ref[start:, :] = project_rows(blocks, weight_ref, rows_ref, sems)
    factor = math.log2(math.e) / math.sqrt(HD)
    x, core, z, y = place[0], place[1], place[2], place[3]
    keys = qkv_ref[:, HD : 2 * HD]
    values = qkv_ref[:, 2 * HD :]
    places = places_short() if short else places_long()
    size = 256
    for b in range(TOKENS // size):
        query = qkv_ref[b * size : (b + 1) * size, :HD]
        scores = lax.dot_general(
            query, keys, (((1,), (1,)), ((), ())), preferred_element_type=jnp.float32
        )
        peak = jnp.max(scores, axis=-1, keepdims=True)
        expo = jnp.exp2((scores - peak) * factor)
        total = jnp.sum(expo, axis=-1, keepdims=True)
        mixed = jnp.dot(expo.astype(jnp.bfloat16), values, preferred_element_type=jnp.float32)
        mixed = (mixed / total).astype(jnp.bfloat16)
        for r in range(size // HALF):
            far, dy, half, other = places[b * (size // HALF) + r]
            owner = 1 - core if other else core
            sign = 1 - 2 * owner
            row = lax.rem(y + sign * dy + 4, 4)
            if short:
                slot = (2 * lax.rem(x + sign * far + 4, 4) + owner) * 4 + row
            else:
                slot = lax.rem(z + sign * far + 8, 8) * 4 + row
            out_ref[slot, half * HALF : (half + 1) * HALF, :] = mixed[r * HALF : (r + 1) * HALF]


def attend(place, done, blocks, weight, short, limit):
    rows = sum(b.shape[0] for b in blocks)
    vmem = pl.BlockSpec(memory_space=pltpu.VMEM)
    return pl.pallas_call(
        functools.partial(attend_kernel, short, len(done)),
        out_shape=jax.ShapeDtypeStruct((TOKENS // 32, 32, HD), jnp.bfloat16),
        in_specs=[pl.BlockSpec(memory_space=pltpu.SMEM)]
        + [vmem] * len(done)
        + [pl.BlockSpec(memory_space=pl.ANY)] * len(blocks)
        + [vmem],
        out_specs=vmem,
        scratch_shapes=[
            pltpu.VMEM((rows, D), jnp.bfloat16),
            pltpu.VMEM((TOKENS, 3 * HD), jnp.bfloat16),
            pltpu.SemaphoreType.DMA((len(blocks),)),
        ],
        compiler_params=pltpu.CompilerParams(vmem_limit_bytes=limit),
        cost_estimate=pl.CostEstimate(
            flops=4 * TOKENS * TOKENS * HD + 6 * rows * D * HD,
            bytes_accessed=2 * rows * D,
            transcendentals=TOKENS * TOKENS,
        ),
    )(place, *done, *blocks, weight)


def weight_kernel(place, weight_ref, out_ref, masked_ref):
    wanted = 2 * place[0] + place[1] == place[2]
    for c in range(3):
        part = weight_ref[c]
        out_ref[:, c * HD : (c + 1) * HD] = part
        masked_ref[:, c * HD : (c + 1) * HD] = jnp.where(wanted, part, jnp.zeros_like(part))


def side_by_side(place, weight):
    out = jax.ShapeDtypeStruct((D, 3 * HD), jnp.bfloat16)
    vmem = pl.BlockSpec(memory_space=pltpu.VMEM)
    return pl.pallas_call(
        weight_kernel,
        out_shape=[out, out],
        in_specs=[pl.BlockSpec(memory_space=pltpu.SMEM), vmem],
        out_specs=[vmem, vmem],
        compiler_params=pltpu.CompilerParams(vmem_limit_bytes=16 * MIB),
        cost_estimate=pl.CostEstimate(flops=0, bytes_accessed=18 * D * HD, transcendentals=0),
    )(place, weight)


def norm(values):
    center = jnp.mean(values, axis=-1, keepdims=True)
    moved = values - center
    spread = jnp.mean(moved * moved, axis=-1, keepdims=True)
    return moved * lax.rsqrt(spread + 1e-05)


def norm_kernel(rows_ref, first_ref, second_ref, whole_ref):
    for n, out_ref in enumerate((first_ref, second_ref)):
        half = norm(rows_ref[n * HALF : (n + 1) * HALF, :]).astype(jnp.bfloat16)
        out_ref[...] = half
        whole_ref[n * HALF : (n + 1) * HALF, :] = half


def layer_norm(rows):
    half = jax.ShapeDtypeStruct((HALF, D), jnp.bfloat16)
    whole = jax.ShapeDtypeStruct((2 * HALF, D), jnp.bfloat16)
    return pl.pallas_call(
        norm_kernel,
        out_shape=[half, half, whole],
        compiler_params=pltpu.CompilerParams(vmem_limit_bytes=8 * MIB),
    )(rows)


def sweep_steps(width, attended_ref, current_ref, store):
    anchor = current_ref[0]
    before = jnp.zeros_like(anchor)
    gap = jnp.zeros_like(anchor)
    for k in range(STEPS):
        current = current_ref[k]
        increment = width[k] * (attended_ref[k].astype(jnp.float32) - current)
        updated = anchor + before
        change = updated - current
        gap = gap + change * change
        store(k, updated, increment)
        before = before + increment
    return jnp.sum(gap)


def sweep_kernel(width, attended_ref, current_ref, normed_ref, gap_ref, updated_ref):
    def store(k, updated, increment):
        updated_ref[k] = updated
        normed_ref[k] = norm(updated).astype(jnp.bfloat16)

    gap = sweep_steps(width, attended_ref, current_ref, store)
    gap_ref[...] = jnp.broadcast_to(gap, gap_ref.shape)


def sweep_update(width, attended, current):
    shape = current.shape
    vmem = pl.BlockSpec(memory_space=pltpu.VMEM)
    return pl.pallas_call(
        sweep_kernel,
        out_shape=[
            jax.ShapeDtypeStruct(shape, jnp.bfloat16),
            jax.ShapeDtypeStruct((1, 1, 128), jnp.float32),
            jax.ShapeDtypeStruct(shape, jnp.float32),
        ],
        in_specs=[pl.BlockSpec(memory_space=pltpu.SMEM)] + [vmem] * 2,
        out_specs=[vmem] * 3,
    )(width, attended, current)


def step_pair(place, far, flip):
    return 2 * lax.rem(place[0] + far, 4) + lax.rem(place[1] + flip, 2)


def last_kernel(width, place, attended_ref, current_ref, first_ref, *refs):
    *piece_refs, marks_ref, advanced_ref = refs

    def store(k, updated, increment):
        advanced_ref[k] = updated + increment

    gap = sweep_steps(width, attended_ref, current_ref, store)
    for n, piece_ref in enumerate(piece_refs):
        piece_ref[...] = advanced_ref[step_pair(place, n // 2, n % 2)]
    marks_ref[:, 0:1, :] = jnp.broadcast_to(first_ref[...], (256, 1, 128))
    marks_ref[:, 1:2, :] = jnp.broadcast_to(gap, (256, 1, 128))


def last_update(width, place, attended, current, first_gap):
    vmem = pl.BlockSpec(memory_space=pltpu.VMEM)
    smem = pl.BlockSpec(memory_space=pltpu.SMEM)
    *pieces, marks = pl.pallas_call(
        last_kernel,
        out_shape=[jax.ShapeDtypeStruct(current.shape[1:], jnp.float32)] * STEPS
        + [jax.ShapeDtypeStruct((256, 2, 128), jnp.float32)],
        in_specs=[smem, smem] + [vmem] * 3,
        out_specs=[vmem] * (STEPS + 1),
        scratch_shapes=[pltpu.VMEM(current.shape, jnp.float32)],
    )(width, place, attended, current, first_gap)
    return pieces, marks


def over_step(pieces):
    return lax.all_to_all(pieces, STEP, split_axis=0, concat_axis=0, tiled=True)


def over_all(pieces):
    return lax.all_to_all(pieces, ALL, split_axis=0, concat_axis=0, tiled=True)


def deliver_kernel(place, *refs):
    *pieces, out_ref = refs
    swapped = place[1] == 1
    for far in range(4):
        same, other = pieces[2 * far][...], pieces[2 * far + 1][...]
        low = jnp.where(swapped, other, same)
        high = jnp.where(swapped, same, other)
        x = lax.rem(place[0] - far + 4, 4)
        out_ref[pl.ds(pl.multiple_of(8 * x, 8), 8), :] = jnp.concatenate([low, high], axis=0)


def deliver(place, pieces):
    got = pieces[:1]
    for n in range(1, STEPS):
        pairs = [
            (2 * i + c, 2 * ((i + n // 2) % 4) + (c + n) % 2) for i in range(4) for c in range(2)
        ]
        got.append(lax.ppermute(pieces[n], STEP, pairs))
    vmem = pl.BlockSpec(memory_space=pltpu.VMEM)
    return pl.pallas_call(
        deliver_kernel,
        out_shape=jax.ShapeDtypeStruct((32, D), jnp.float32),
        in_specs=[pl.BlockSpec(memory_space=pltpu.SMEM)] + [vmem] * STEPS,
        out_specs=vmem,
    )(place, *got)


def local(step_index, window_init, qkv_weight):
    window = window_init[0]
    place = jnp.stack([lax.axis_index(a) for a in ALL]).astype(jnp.int32)
    width = (step_index[:-1] - step_index[1:]).astype(jnp.float32) / 1000.0
    weights = side_by_side(place, qkv_weight)
    groups, start, (weight, masked) = gather_long(layer_norm(window), window, weights)
    other_weight = lax.psum(masked, "z")
    done = [project(group, weight, 24 * MIB) for group in groups[:-1]]
    attended = attend(place, done, groups[-1], weight, False, 24 * MIB)
    pieces = attended.reshape(32, STEPS, 4, HD).transpose(1, 0, 2, 3)
    got = over_all(pieces.reshape(256, 4, HD)).reshape(STEPS, HEADS, 4, HD)
    attended = got.transpose(0, 2, 1, 3).reshape(STEPS, 4, D)
    normed, first_gap, updated = sweep_update(width, attended, start)

    rows = lax.all_to_all(normed, "z", split_axis=0, concat_axis=0, tiled=True).reshape(32, D)
    done, blocks, other_weight = project_short(rows, other_weight)
    attended = attend(place, done, blocks, other_weight, True, 20 * MIB)
    pieces = attended.reshape(STEPS, 4, 8, 4, HD).transpose(0, 2, 1, 3, 4)
    got = over_all(pieces.reshape(256, 4, HD)).reshape(8, STEPS, 4, 4, HD)
    attended = got.transpose(1, 3, 0, 2, 4).reshape(STEPS, 4, D)
    pieces, marks = last_update(width, place, attended, updated, first_gap)
    totals = jnp.sum(over_all(marks), axis=0)[:, 0]
    residuals = jnp.sqrt(totals / (STEPS * TOKENS * D))
    return (deliver(place, pieces)[None], residuals)


def solution(mesh):
    fine = Mesh(mesh.devices.reshape(4, 2, 8, 4), ALL)
    placed = (P(), P(STEP, SEQ, None), P(None, None, SEQ))
    return jax.shard_map(
        local, mesh=fine, in_specs=placed, out_specs=(P(STEP, SEQ, None), P()), check_vma=False
    )
```

```python
import functools
import math

import jax
import jax.numpy as jnp
from jax import lax
from jax.experimental import pallas as pl
from jax.experimental.pallas import tpu as pltpu
from jax.sharding import Mesh, PartitionSpec as P

HD = 128
HEADS = 32
D = HEADS * HD
STEPS = 8
TOKENS = 1024
SIZES = {"x": 4, "c": 2, "z": 8, "y": 4}
STEP = ("x", "c")
SEQ = ("z", "y")
ALL = STEP + SEQ
HALF = 16
MIB = 1024 * 1024


def shift(x, axis, by):
    n = SIZES[axis]
    pairs = []
    for i in range(n):
        if axis == "x":
            pairs += [(2 * i, 2 * ((i + by) % n)), (2 * i + 1, 2 * ((i - by) % n) + 1)]
        else:
            pairs += [(i, (i + by) % n), (n + i, n + (i - by) % n)]
    return lax.ppermute(x, ("x", "c") if axis == "x" else ("c", axis), pairs)


def swap(x):
    return lax.ppermute(x, "c", [(0, 1), (1, 0)])


def join_kernel(ranges, *refs):
    *blocks, out_ref = refs
    start = 0
    for block, (low, high) in zip(blocks, ranges):
        out_ref[start : start + high - low, :] = block[low:high, :]
        start += high - low


def join(blocks, ranges=None):
    ranges = ranges or [(0, b.shape[0]) for b in blocks]
    rows = sum(high - low for low, high in ranges)
    return pl.pallas_call(
        functools.partial(join_kernel, ranges),
        out_shape=jax.ShapeDtypeStruct((rows, D), jnp.bfloat16),
        in_specs=[pl.BlockSpec(memory_space=pltpu.VMEM)] * len(blocks),
        out_specs=pl.BlockSpec(memory_space=pltpu.VMEM),
        compiler_params=pltpu.CompilerParams(vmem_limit_bytes=8 * MIB),
        cost_estimate=pl.CostEstimate(flops=0, bytes_accessed=4 * rows * D, transcendentals=0),
    )(*blocks)


SMALL_4 = (0, -1, 1, -2)
SMALL_Z = (0, -4, -1, -5, 1, -3, 2, -2)


def small_4(x, axis):
    return join([x, shift(x, axis, 1), shift(x, axis, -1), shift(x, axis, 2)])


def tie(*values):
    return lax.optimization_barrier(values)


def both_ways(up, down, axis):
    return tie(shift(up, axis, 1), shift(down, axis, -1))


def ring_of_4(x, axis):
    up, down = both_ways(x, x, axis)
    return {0: x, -1: up, 1: down, -2: shift(up, axis, 1)}


LONG = (
    ((0, -1, 1), (0,)),
    ((-2, 2), (-1, 1)),
    ((-3, 3), (-2,)),
)


def small_long(first, second, whole):
    near = [shift(first, "y", 1), shift(first, "y", -1), shift(first, "y", 2)]
    far = shift(whole, "z", 4)
    pair = join([second, far], [(0, HALF), (HALF, 2 * HALF)])
    others = [shift(pair, "z", 1), shift(pair, "z", -1), shift(pair, "z", -2)]
    near_z = join([pair, *others, far], [(0, 2 * HALF)] * 4 + [(0, HALF)])
    return join([first, *near]), near_z


def gather_long(halves, window, weights):
    near_y, near_z = small_long(*halves)
    by_z = {0: near_y}
    up, down = both_ways(near_y, near_y, "z")
    window = over_step(window.reshape(STEPS, 4, D))
    by_z[-1], by_z[1] = up, down
    up, down, window, *weights = tie(*both_ways(up, down, "z"), window, *weights)
    by_z[-2], by_z[2] = up, down
    by_z[-3], by_z[3] = both_ways(up, down, "z")
    up, down = both_ways(near_z, near_z, "y")
    by_y = {0: near_z, -1: up, 1: down}
    by_z[-2], up = tie(by_z[-2], up)
    by_y[-2] = shift(up, "y", 1)
    groups = [[by_z[d] for d in zs] + [by_y[d] for d in ys] for zs, ys in LONG]
    return groups, window, weights


def places_long():
    places = []
    for far_z, far_y in LONG:
        places += [(dz, dy, 0, 0) for dz in far_z for dy in SMALL_4]
        for dy in far_y:
            places += [(dz, dy, 1, 0) for dz in SMALL_Z] + [(-4, dy, 0, 0)]
    return places


NEAR, FAR = (0, -1, 1), (-2,)


def project_short(x, weight):
    near_y, near_x = tie(small_4(x[:HALF], "y"), small_4(x[HALF:], "x"))
    up, down, weight = tie(*both_ways(near_y, near_y, "x"), weight)
    by_x = {0: near_y, -1: up, 1: down, -2: shift(up, "x", 1)}
    by_y = ring_of_4(near_x, "y")
    near = [by_x[d] for d in NEAR] + [by_y[d] for d in NEAR]
    done = project(near + [swap(b) for b in near], weight, 16 * MIB)
    far = [by_x[d] for d in FAR] + [by_y[d] for d in FAR]
    *far, done = tie(*far, done)
    return [done], far + [swap(b) for b in far], weight


def places_short():
    places = []
    for far in (NEAR, FAR):
        for core in (0, 1):
            places += [(dx, dy, 0, core) for dx in far for dy in SMALL_4]
            places += [(dx, dy, 1, core) for dy in far for dx in SMALL_4]
    return places


def project_rows(blocks, weight_ref, rows_ref, sems):
    copies = []
    start = 0
    for n, block in enumerate(blocks):
        rows = block.shape[0]
        copies.append(
            pltpu.make_async_copy(block, rows_ref.at[pl.ds(start, rows), :], sems.at[n])
        )
        copies[-1].start()
        start += rows
    for copy in copies:
        copy.wait()
    out = jnp.dot(rows_ref[...], weight_ref[...], preferred_element_type=jnp.float32)
    return out.astype(jnp.bfloat16)


def project_kernel(*refs):
    *blocks, weight_ref, out_ref, rows_ref, sems = refs
    out_ref[...] = project_rows(blocks, weight_ref, rows_ref, sems)


def project(blocks, weight, limit):
    rows = sum(b.shape[0] for b in blocks)
    vmem = pl.BlockSpec(memory_space=pltpu.VMEM)
    return pl.pallas_call(
        project_kernel,
        out_shape=jax.ShapeDtypeStruct((rows, 3 * HD), jnp.bfloat16),
        in_specs=[pl.BlockSpec(memory_space=pl.ANY)] * len(blocks) + [vmem],
        out_specs=vmem,
        scratch_shapes=[
            pltpu.VMEM((rows, D), jnp.bfloat16),
            pltpu.SemaphoreType.DMA((len(blocks),)),
        ],
        compiler_params=pltpu.CompilerParams(vmem_limit_bytes=limit),
        cost_estimate=pl.CostEstimate(
            flops=6 * rows * D * HD, bytes_accessed=2 * rows * D, transcendentals=0
        ),
    )(*blocks, weight)


def attend_kernel(short, ready, place, *refs):
    *blocks, weight_ref, out_ref, rows_ref, qkv_ref, sems = refs
    blocks, done = blocks[ready:], blocks[:ready]
    start = 0
    for part in done:
        qkv_ref[start : start + part.shape[0], :] = part[...]
        start += part.shape[0]
    qkv_ref[start:, :] = project_rows(blocks, weight_ref, rows_ref, sems)
    factor = math.log2(math.e) / math.sqrt(HD)
    x, core, z, y = place[0], place[1], place[2], place[3]
    keys = qkv_ref[:, HD : 2 * HD]
    values = qkv_ref[:, 2 * HD :]
    places = places_short() if short else places_long()
    size = 256
    for b in range(TOKENS // size):
        query = qkv_ref[b * size : (b + 1) * size, :HD]
        scores = lax.dot_general(
            query, keys, (((1,), (1,)), ((), ())), preferred_element_type=jnp.float32
        )
        peak = jnp.max(scores, axis=-1, keepdims=True)
        expo = jnp.exp2((scores - peak) * factor)
        total = jnp.sum(expo, axis=-1, keepdims=True)
        mixed = jnp.dot(expo.astype(jnp.bfloat16), values, preferred_element_type=jnp.float32)
        mixed = (mixed / total).astype(jnp.bfloat16)
        for r in range(size // HALF):
            far, dy, half, other = places[b * (size // HALF) + r]
            owner = 1 - core if other else core
            sign = 1 - 2 * owner
            row = lax.rem(y + sign * dy + 4, 4)
            if short:
                slot = (2 * lax.rem(x + sign * far + 4, 4) + owner) * 4 + row
            else:
                slot = lax.rem(z + sign * far + 8, 8) * 4 + row
            out_ref[slot, half * HALF : (half + 1) * HALF, :] = mixed[r * HALF : (r + 1) * HALF]


def attend(place, done, blocks, weight, short, limit):
    rows = sum(b.shape[0] for b in blocks)
    vmem = pl.BlockSpec(memory_space=pltpu.VMEM)
    return pl.pallas_call(
        functools.partial(attend_kernel, short, len(done)),
        out_shape=jax.ShapeDtypeStruct((TOKENS // 32, 32, HD), jnp.bfloat16),
        in_specs=[pl.BlockSpec(memory_space=pltpu.SMEM)]
        + [vmem] * len(done)
        + [pl.BlockSpec(memory_space=pl.ANY)] * len(blocks)
        + [vmem],
        out_specs=vmem,
        scratch_shapes=[
            pltpu.VMEM((rows, D), jnp.bfloat16),
            pltpu.VMEM((TOKENS, 3 * HD), jnp.bfloat16),
            pltpu.SemaphoreType.DMA((len(blocks),)),
        ],
        compiler_params=pltpu.CompilerParams(vmem_limit_bytes=limit),
        cost_estimate=pl.CostEstimate(
            flops=4 * TOKENS * TOKENS * HD + 6 * rows * D * HD,
            bytes_accessed=2 * rows * D,
            transcendentals=TOKENS * TOKENS,
        ),
    )(place, *done, *blocks, weight)


def weight_kernel(place, weight_ref, out_ref, masked_ref):
    wanted = 2 * place[0] + place[1] == place[2]
    for c in range(3):
        part = weight_ref[c]
        out_ref[:, c * HD : (c + 1) * HD] = part
        masked_ref[:, c * HD : (c + 1) * HD] = jnp.where(wanted, part, jnp.zeros_like(part))


def side_by_side(place, weight):
    out = jax.ShapeDtypeStruct((D, 3 * HD), jnp.bfloat16)
    vmem = pl.BlockSpec(memory_space=pltpu.VMEM)
    return pl.pallas_call(
        weight_kernel,
        out_shape=[out, out],
        in_specs=[pl.BlockSpec(memory_space=pltpu.SMEM), vmem],
        out_specs=[vmem, vmem],
        compiler_params=pltpu.CompilerParams(vmem_limit_bytes=16 * MIB),
        cost_estimate=pl.CostEstimate(flops=0, bytes_accessed=18 * D * HD, transcendentals=0),
    )(place, weight)


def norm(values):
    center = jnp.mean(values, axis=-1, keepdims=True)
    moved = values - center
    spread = jnp.mean(moved * moved, axis=-1, keepdims=True)
    return moved * lax.rsqrt(spread + 1e-05)


def norm_kernel(rows_ref, first_ref, second_ref, whole_ref):
    for n, out_ref in enumerate((first_ref, second_ref)):
        half = norm(rows_ref[n * HALF : (n + 1) * HALF, :]).astype(jnp.bfloat16)
        out_ref[...] = half
        whole_ref[n * HALF : (n + 1) * HALF, :] = half


def layer_norm(rows):
    half = jax.ShapeDtypeStruct((HALF, D), jnp.bfloat16)
    whole = jax.ShapeDtypeStruct((2 * HALF, D), jnp.bfloat16)
    return pl.pallas_call(
        norm_kernel,
        out_shape=[half, half, whole],
        compiler_params=pltpu.CompilerParams(vmem_limit_bytes=8 * MIB),
    )(rows)


def sweep_steps(width, attended_ref, current_ref, store):
    anchor = current_ref[0]
    before = jnp.zeros_like(anchor)
    gap = jnp.zeros_like(anchor)
    for k in range(STEPS):
        current = current_ref[k]
        increment = width[k] * (attended_ref[k].astype(jnp.float32) - current)
        updated = anchor + before
        change = updated - current
        gap = gap + change * change
        store(k, updated, increment)
        before = before + increment
    return jnp.sum(gap)


def sweep_kernel(width, attended_ref, current_ref, normed_ref, gap_ref, updated_ref):
    def store(k, updated, increment):
        updated_ref[k] = updated
        normed_ref[k] = norm(updated).astype(jnp.bfloat16)

    gap = sweep_steps(width, attended_ref, current_ref, store)
    gap_ref[...] = jnp.broadcast_to(gap, gap_ref.shape)


def sweep_update(width, attended, current):
    shape = current.shape
    vmem = pl.BlockSpec(memory_space=pltpu.VMEM)
    return pl.pallas_call(
        sweep_kernel,
        out_shape=[
            jax.ShapeDtypeStruct(shape, jnp.bfloat16),
            jax.ShapeDtypeStruct((1, 1, 128), jnp.float32),
            jax.ShapeDtypeStruct(shape, jnp.float32),
        ],
        in_specs=[pl.BlockSpec(memory_space=pltpu.SMEM)] + [vmem] * 2,
        out_specs=[vmem] * 3,
    )(width, attended, current)


def step_pair(place, far, flip):
    return 2 * lax.rem(place[0] + far, 4) + lax.rem(place[1] + flip, 2)


def last_kernel(width, place, attended_ref, current_ref, first_ref, *refs):
    *piece_refs, marks_ref, advanced_ref = refs

    def store(k, updated, increment):
        advanced_ref[k] = updated + increment

    gap = sweep_steps(width, attended_ref, current_ref, store)
    for n, piece_ref in enumerate(piece_refs):
        piece_ref[...] = advanced_ref[step_pair(place, n // 2, n % 2)]
    marks_ref[:, 0:1, :] = jnp.broadcast_to(first_ref[...], (256, 1, 128))
    marks_ref[:, 1:2, :] = jnp.broadcast_to(gap, (256, 1, 128))


def last_update(width, place, attended, current, first_gap):
    vmem = pl.BlockSpec(memory_space=pltpu.VMEM)
    smem = pl.BlockSpec(memory_space=pltpu.SMEM)
    *pieces, marks = pl.pallas_call(
        last_kernel,
        out_shape=[jax.ShapeDtypeStruct(current.shape[1:], jnp.float32)] * STEPS
        + [jax.ShapeDtypeStruct((256, 2, 128), jnp.float32)],
        in_specs=[smem, smem] + [vmem] * 3,
        out_specs=[vmem] * (STEPS + 1),
        scratch_shapes=[pltpu.VMEM(current.shape, jnp.float32)],
    )(width, place, attended, current, first_gap)
    return pieces, marks


def over_step(pieces):
    return lax.all_to_all(pieces, STEP, split_axis=0, concat_axis=0, tiled=True)


def over_all(pieces):
    return lax.all_to_all(pieces, ALL, split_axis=0, concat_axis=0, tiled=True)


def deliver_kernel(place, *refs):
    *pieces, out_ref = refs
    swapped = place[1] == 1
    for far in range(4):
        same, other = pieces[2 * far][...], pieces[2 * far + 1][...]
        low = jnp.where(swapped, other, same)
        high = jnp.where(swapped, same, other)
        x = lax.rem(place[0] - far + 4, 4)
        out_ref[pl.ds(pl.multiple_of(8 * x, 8), 8), :] = jnp.concatenate([low, high], axis=0)


def deliver(place, pieces):
    got = pieces[:1]
    for n in range(1, STEPS):
        pairs = [
            (2 * i + c, 2 * ((i + n // 2) % 4) + (c + n) % 2) for i in range(4) for c in range(2)
        ]
        got.append(lax.ppermute(pieces[n], STEP, pairs))
    vmem = pl.BlockSpec(memory_space=pltpu.VMEM)
    return pl.pallas_call(
        deliver_kernel,
        out_shape=jax.ShapeDtypeStruct((32, D), jnp.float32),
        in_specs=[pl.BlockSpec(memory_space=pltpu.SMEM)] + [vmem] * STEPS,
        out_specs=vmem,
    )(place, *got)


def local(step_index, window_init, qkv_weight):
    window = window_init[0]
    place = jnp.stack([lax.axis_index(a) for a in ALL]).astype(jnp.int32)
    width = (step_index[:-1] - step_index[1:]).astype(jnp.float32) / 1000.0
    weights = side_by_side(place, qkv_weight)
    groups, start, (weight, masked) = gather_long(layer_norm(window), window, weights)
    other_weight = lax.psum(masked, "z")
    done = [project(group, weight, 24 * MIB) for group in groups[:-1]]
    attended = attend(place, done, groups[-1], weight, False, 24 * MIB)
    pieces = attended.reshape(32, STEPS, 4, HD).transpose(1, 0, 2, 3)
    got = over_all(pieces.reshape(256, 4, HD)).reshape(STEPS, HEADS, 4, HD)
    attended = got.transpose(0, 2, 1, 3).reshape(STEPS, 4, D)
    normed, first_gap, updated = sweep_update(width, attended, start)

    rows = lax.all_to_all(normed, "z", split_axis=0, concat_axis=0, tiled=True).reshape(32, D)
    done, blocks, other_weight = project_short(rows, other_weight)
    attended = attend(place, done, blocks, other_weight, True, 20 * MIB)
    pieces = attended.reshape(STEPS, 4, 8, 4, HD).transpose(0, 2, 1, 3, 4)
    got = over_all(pieces.reshape(256, 4, HD)).reshape(8, STEPS, 4, 4, HD)
    attended = got.transpose(1, 3, 0, 2, 4).reshape(STEPS, 4, D)
    pieces, marks = last_update(width, place, attended, updated, first_gap)
    totals = jnp.sum(over_all(marks), axis=0)[:, 0]
    residuals = jnp.sqrt(totals / (STEPS * TOKENS * D))
    return (deliver(place, pieces)[None], residuals)


def solution(mesh):
    fine = Mesh(mesh.devices.reshape(4, 2, 8, 4), ALL)
    placed = (P(), P(STEP, SEQ, None), P(None, None, SEQ))
    return jax.shard_map(
        local, mesh=fine, in_specs=placed, out_specs=(P(STEP, SEQ, None), P()), check_vma=False
    )
```

```python
import functools
import math

import jax
import jax.numpy as jnp
from jax import lax
from jax.experimental import pallas as pl
from jax.experimental.pallas import tpu as pltpu
from jax.sharding import Mesh, PartitionSpec as P

HD = 128
HEADS = 32
D = HEADS * HD
STEPS = 8
TOKENS = 1024
SIZES = {"x": 4, "c": 2, "z": 8, "y": 4}
STEP = ("x", "c")
SEQ = ("z", "y")
ALL = STEP + SEQ
HALF = 16
MIB = 1024 * 1024


def shift(x, axis, by):
    n = SIZES[axis]
    pairs = []
    for i in range(n):
        if axis == "x":
            pairs += [(2 * i, 2 * ((i + by) % n)), (2 * i + 1, 2 * ((i - by) % n) + 1)]
        else:
            pairs += [(i, (i + by) % n), (n + i, n + (i - by) % n)]
    return lax.ppermute(x, ("x", "c") if axis == "x" else ("c", axis), pairs)


def swap(x):
    return lax.ppermute(x, "c", [(0, 1), (1, 0)])


def join_kernel(ranges, *refs):
    *blocks, out_ref = refs
    start = 0
    for block, (low, high) in zip(blocks, ranges):
        out_ref[start : start + high - low, :] = block[low:high, :]
        start += high - low


def join(blocks, ranges=None):
    ranges = ranges or [(0, b.shape[0]) for b in blocks]
    rows = sum(high - low for low, high in ranges)
    return pl.pallas_call(
        functools.partial(join_kernel, ranges),
        out_shape=jax.ShapeDtypeStruct((rows, D), jnp.bfloat16),
        in_specs=[pl.BlockSpec(memory_space=pltpu.VMEM)] * len(blocks),
        out_specs=pl.BlockSpec(memory_space=pltpu.VMEM),
        compiler_params=pltpu.CompilerParams(vmem_limit_bytes=8 * MIB),
        cost_estimate=pl.CostEstimate(flops=0, bytes_accessed=4 * rows * D, transcendentals=0),
    )(*blocks)


SMALL_4 = (0, -1, 1, -2)
SMALL_Z = (0, -4, -1, -5, 1, -3, 2, -2)


def small_4(x, axis):
    return join([x, shift(x, axis, 1), shift(x, axis, -1), shift(x, axis, 2)])


def tie(*values):
    return lax.optimization_barrier(values)


def both_ways(up, down, axis):
    return tie(shift(up, axis, 1), shift(down, axis, -1))


def ring_of_4(x, axis):
    up, down = both_ways(x, x, axis)
    return {0: x, -1: up, 1: down, -2: shift(up, axis, 1)}


LONG = (
    ((0, -1, 1), (0,)),
    ((-2, 2), (-1, 1)),
    ((-3, 3), (-2,)),
)


def small_long(first, second, whole):
    near = [shift(first, "y", 1), shift(first, "y", -1), shift(first, "y", 2)]
    far, *near = tie(shift(whole, "z", 4), *near)
    pair = join([second, far], [(0, HALF), (HALF, 2 * HALF)])
    near_y, pair = tie(join([first, *near]), pair)
    others = [shift(pair, "z", 1), shift(pair, "z", -1), shift(pair, "z", -2)]
    near_z = join([pair, *others, far], [(0, 2 * HALF)] * 4 + [(0, HALF)])
    return near_y, near_z


def gather_long(halves, window, weights):
    near_y, near_z = small_long(*halves)
    by_z = {0: near_y}
    up, down = both_ways(near_y, near_y, "z")
    window = over_step(window.reshape(STEPS, 4, D))
    by_z[-1], by_z[1] = up, down
    up, down, window, *weights = tie(*both_ways(up, down, "z"), window, *weights)
    by_z[-2], by_z[2] = up, down
    by_z[-3], by_z[3] = both_ways(up, down, "z")
    up, down = both_ways(near_z, near_z, "y")
    by_y = {0: near_z, -1: up, 1: down}
    by_z[-3], up = tie(by_z[-3], up)
    by_y[-2] = shift(up, "y", 1)
    groups = [[by_z[d] for d in zs] + [by_y[d] for d in ys] for zs, ys in LONG]
    return groups, window, weights


def places_long():
    places = []
    for far_z, far_y in LONG:
        places += [(dz, dy, 0, 0) for dz in far_z for dy in SMALL_4]
        for dy in far_y:
            places += [(dz, dy, 1, 0) for dz in SMALL_Z] + [(-4, dy, 0, 0)]
    return places


NEAR, FAR = (0, -1, 1), (-2,)


def project_short(x, weight):
    near_y, near_x = tie(small_4(x[:HALF], "y"), small_4(x[HALF:], "x"))
    up, down, weight = tie(*both_ways(near_y, near_y, "x"), weight)
    by_x = {0: near_y, -1: up, 1: down, -2: shift(up, "x", 1)}
    by_y = ring_of_4(near_x, "y")
    near = [by_x[d] for d in NEAR] + [by_y[d] for d in NEAR]
    done = project(near + [swap(b) for b in near], weight, 16 * MIB)
    far = [by_x[d] for d in FAR] + [by_y[d] for d in FAR]
    *far, done = tie(*far, done)
    return [done], far + [swap(b) for b in far], weight


def places_short():
    places = []
    for far in (NEAR, FAR):
        for core in (0, 1):
            places += [(dx, dy, 0, core) for dx in far for dy in SMALL_4]
            places += [(dx, dy, 1, core) for dy in far for dx in SMALL_4]
    return places


def project_rows(blocks, weight_ref, rows_ref, sems):
    copies = []
    start = 0
    for n, block in enumerate(blocks):
        rows = block.shape[0]
        copies.append(
            pltpu.make_async_copy(block, rows_ref.at[pl.ds(start, rows), :], sems.at[n])
        )
        copies[-1].start()
        start += rows
    for copy in copies:
        copy.wait()
    out = jnp.dot(rows_ref[...], weight_ref[...], preferred_element_type=jnp.float32)
    return out.astype(jnp.bfloat16)


def project_kernel(*refs):
    *blocks, weight_ref, out_ref, rows_ref, sems = refs
    out_ref[...] = project_rows(blocks, weight_ref, rows_ref, sems)


def project(blocks, weight, limit):
    rows = sum(b.shape[0] for b in blocks)
    vmem = pl.BlockSpec(memory_space=pltpu.VMEM)
    return pl.pallas_call(
        project_kernel,
        out_shape=jax.ShapeDtypeStruct((rows, 3 * HD), jnp.bfloat16),
        in_specs=[pl.BlockSpec(memory_space=pl.ANY)] * len(blocks) + [vmem],
        out_specs=vmem,
        scratch_shapes=[
            pltpu.VMEM((rows, D), jnp.bfloat16),
            pltpu.SemaphoreType.DMA((len(blocks),)),
        ],
        compiler_params=pltpu.CompilerParams(vmem_limit_bytes=limit),
        cost_estimate=pl.CostEstimate(
            flops=6 * rows * D * HD, bytes_accessed=2 * rows * D, transcendentals=0
        ),
    )(*blocks, weight)


def attend_kernel(short, ready, place, *refs):
    *blocks, weight_ref, out_ref, rows_ref, qkv_ref, sems = refs
    blocks, done = blocks[ready:], blocks[:ready]
    start = 0
    for part in done:
        qkv_ref[start : start + part.shape[0], :] = part[...]
        start += part.shape[0]
    qkv_ref[start:, :] = project_rows(blocks, weight_ref, rows_ref, sems)
    factor = math.log2(math.e) / math.sqrt(HD)
    x, core, z, y = place[0], place[1], place[2], place[3]
    keys = qkv_ref[:, HD : 2 * HD]
    values = qkv_ref[:, 2 * HD :]
    places = places_short() if short else places_long()
    size = 256
    for b in range(TOKENS // size):
        query = qkv_ref[b * size : (b + 1) * size, :HD]
        scores = lax.dot_general(
            query, keys, (((1,), (1,)), ((), ())), preferred_element_type=jnp.float32
        )
        peak = jnp.max(scores, axis=-1, keepdims=True)
        expo = jnp.exp2((scores - peak) * factor)
        total = jnp.sum(expo, axis=-1, keepdims=True)
        mixed = jnp.dot(expo.astype(jnp.bfloat16), values, preferred_element_type=jnp.float32)
        mixed = (mixed / total).astype(jnp.bfloat16)
        for r in range(size // HALF):
            far, dy, half, other = places[b * (size // HALF) + r]
            owner = 1 - core if other else core
            sign = 1 - 2 * owner
            row = lax.rem(y + sign * dy + 4, 4)
            if short:
                slot = (2 * lax.rem(x + sign * far + 4, 4) + owner) * 4 + row
            else:
                slot = lax.rem(z + sign * far + 8, 8) * 4 + row
            out_ref[slot, half * HALF : (half + 1) * HALF, :] = mixed[r * HALF : (r + 1) * HALF]


def attend(place, done, blocks, weight, short, limit):
    rows = sum(b.shape[0] for b in blocks)
    vmem = pl.BlockSpec(memory_space=pltpu.VMEM)
    return pl.pallas_call(
        functools.partial(attend_kernel, short, len(done)),
        out_shape=jax.ShapeDtypeStruct((TOKENS // 32, 32, HD), jnp.bfloat16),
        in_specs=[pl.BlockSpec(memory_space=pltpu.SMEM)]
        + [vmem] * len(done)
        + [pl.BlockSpec(memory_space=pl.ANY)] * len(blocks)
        + [vmem],
        out_specs=vmem,
        scratch_shapes=[
            pltpu.VMEM((rows, D), jnp.bfloat16),
            pltpu.VMEM((TOKENS, 3 * HD), jnp.bfloat16),
            pltpu.SemaphoreType.DMA((len(blocks),)),
        ],
        compiler_params=pltpu.CompilerParams(vmem_limit_bytes=limit),
        cost_estimate=pl.CostEstimate(
            flops=4 * TOKENS * TOKENS * HD + 6 * rows * D * HD,
            bytes_accessed=2 * rows * D,
            transcendentals=TOKENS * TOKENS,
        ),
    )(place, *done, *blocks, weight)


def weight_kernel(place, weight_ref, out_ref, masked_ref):
    wanted = 2 * place[0] + place[1] == place[2]
    for c in range(3):
        part = weight_ref[c]
        out_ref[:, c * HD : (c + 1) * HD] = part
        masked_ref[:, c * HD : (c + 1) * HD] = jnp.where(wanted, part, jnp.zeros_like(part))


def side_by_side(place, weight):
    out = jax.ShapeDtypeStruct((D, 3 * HD), jnp.bfloat16)
    vmem = pl.BlockSpec(memory_space=pltpu.VMEM)
    return pl.pallas_call(
        weight_kernel,
        out_shape=[out, out],
        in_specs=[pl.BlockSpec(memory_space=pltpu.SMEM), vmem],
        out_specs=[vmem, vmem],
        compiler_params=pltpu.CompilerParams(vmem_limit_bytes=16 * MIB),
        cost_estimate=pl.CostEstimate(flops=0, bytes_accessed=18 * D * HD, transcendentals=0),
    )(place, weight)


def norm(values):
    center = jnp.mean(values, axis=-1, keepdims=True)
    moved = values - center
    spread = jnp.mean(moved * moved, axis=-1, keepdims=True)
    return moved * lax.rsqrt(spread + 1e-05)


def norm_kernel(rows_ref, first_ref, second_ref, whole_ref):
    for n, out_ref in enumerate((first_ref, second_ref)):
        half = norm(rows_ref[n * HALF : (n + 1) * HALF, :]).astype(jnp.bfloat16)
        out_ref[...] = half
        whole_ref[n * HALF : (n + 1) * HALF, :] = half


def layer_norm(rows):
    half = jax.ShapeDtypeStruct((HALF, D), jnp.bfloat16)
    whole = jax.ShapeDtypeStruct((2 * HALF, D), jnp.bfloat16)
    return pl.pallas_call(
        norm_kernel,
        out_shape=[half, half, whole],
        compiler_params=pltpu.CompilerParams(vmem_limit_bytes=8 * MIB),
    )(rows)


def sweep_steps(width, attended_ref, current_ref, store):
    anchor = current_ref[0]
    before = jnp.zeros_like(anchor)
    gap = jnp.zeros_like(anchor)
    for k in range(STEPS):
        current = current_ref[k]
        increment = width[k] * (attended_ref[k].astype(jnp.float32) - current)
        updated = anchor + before
        change = updated - current
        gap = gap + change * change
        store(k, updated, increment)
        before = before + increment
    return jnp.sum(gap)


def sweep_kernel(width, attended_ref, current_ref, normed_ref, gap_ref, updated_ref):
    def store(k, updated, increment):
        updated_ref[k] = updated
        normed_ref[k] = norm(updated).astype(jnp.bfloat16)

    gap = sweep_steps(width, attended_ref, current_ref, store)
    gap_ref[...] = jnp.broadcast_to(gap, gap_ref.shape)


def sweep_update(width, attended, current):
    shape = current.shape
    vmem = pl.BlockSpec(memory_space=pltpu.VMEM)
    return pl.pallas_call(
        sweep_kernel,
        out_shape=[
            jax.ShapeDtypeStruct(shape, jnp.bfloat16),
            jax.ShapeDtypeStruct((1, 1, 128), jnp.float32),
            jax.ShapeDtypeStruct(shape, jnp.float32),
        ],
        in_specs=[pl.BlockSpec(memory_space=pltpu.SMEM)] + [vmem] * 2,
        out_specs=[vmem] * 3,
    )(width, attended, current)


def step_pair(place, far, flip):
    return 2 * lax.rem(place[0] + far, 4) + lax.rem(place[1] + flip, 2)


def last_kernel(width, place, attended_ref, current_ref, first_ref, *refs):
    *piece_refs, marks_ref, advanced_ref = refs

    def store(k, updated, increment):
        advanced_ref[k] = updated + increment

    gap = sweep_steps(width, attended_ref, current_ref, store)
    for n, piece_ref in enumerate(piece_refs):
        piece_ref[...] = advanced_ref[step_pair(place, n // 2, n % 2)]
    marks_ref[:, 0:1, :] = jnp.broadcast_to(first_ref[...], (256, 1, 128))
    marks_ref[:, 1:2, :] = jnp.broadcast_to(gap, (256, 1, 128))


def last_update(width, place, attended, current, first_gap):
    vmem = pl.BlockSpec(memory_space=pltpu.VMEM)
    smem = pl.BlockSpec(memory_space=pltpu.SMEM)
    *pieces, marks = pl.pallas_call(
        last_kernel,
        out_shape=[jax.ShapeDtypeStruct(current.shape[1:], jnp.float32)] * STEPS
        + [jax.ShapeDtypeStruct((256, 2, 128), jnp.float32)],
        in_specs=[smem, smem] + [vmem] * 3,
        out_specs=[vmem] * (STEPS + 1),
        scratch_shapes=[pltpu.VMEM(current.shape, jnp.float32)],
    )(width, place, attended, current, first_gap)
    return pieces, marks


def over_step(pieces):
    return lax.all_to_all(pieces, STEP, split_axis=0, concat_axis=0, tiled=True)


def over_all(pieces):
    return lax.all_to_all(pieces, ALL, split_axis=0, concat_axis=0, tiled=True)


def deliver_kernel(place, *refs):
    *pieces, out_ref = refs
    swapped = place[1] == 1
    for far in range(4):
        same, other = pieces[2 * far][...], pieces[2 * far + 1][...]
        low = jnp.where(swapped, other, same)
        high = jnp.where(swapped, same, other)
        x = lax.rem(place[0] - far + 4, 4)
        out_ref[pl.ds(pl.multiple_of(8 * x, 8), 8), :] = jnp.concatenate([low, high], axis=0)


def deliver(place, pieces):
    got = pieces[:1]
    for n in range(1, STEPS):
        pairs = [
            (2 * i + c, 2 * ((i + n // 2) % 4) + (c + n) % 2) for i in range(4) for c in range(2)
        ]
        got.append(lax.ppermute(pieces[n], STEP, pairs))
    vmem = pl.BlockSpec(memory_space=pltpu.VMEM)
    return pl.pallas_call(
        deliver_kernel,
        out_shape=jax.ShapeDtypeStruct((32, D), jnp.float32),
        in_specs=[pl.BlockSpec(memory_space=pltpu.SMEM)] + [vmem] * STEPS,
        out_specs=vmem,
    )(place, *got)


def local(step_index, window_init, qkv_weight):
    window = window_init[0]
    place = jnp.stack([lax.axis_index(a) for a in ALL]).astype(jnp.int32)
    width = (step_index[:-1] - step_index[1:]).astype(jnp.float32) / 1000.0
    weights = side_by_side(place, qkv_weight)
    groups, start, (weight, masked) = gather_long(layer_norm(window), window, weights)
    other_weight = lax.psum(masked, "z")
    done = [project(group, weight, 24 * MIB) for group in groups[:-1]]
    attended = attend(place, done, groups[-1], weight, False, 24 * MIB)
    pieces = attended.reshape(32, STEPS, 4, HD).transpose(1, 0, 2, 3)
    got = over_all(pieces.reshape(256, 4, HD)).reshape(STEPS, HEADS, 4, HD)
    attended = got.transpose(0, 2, 1, 3).reshape(STEPS, 4, D)
    normed, first_gap, updated = sweep_update(width, attended, start)

    rows = lax.all_to_all(normed, "z", split_axis=0, concat_axis=0, tiled=True).reshape(32, D)
    done, blocks, other_weight = project_short(rows, other_weight)
    attended = attend(place, done, blocks, other_weight, True, 20 * MIB)
    pieces = attended.reshape(STEPS, 4, 8, 4, HD).transpose(0, 2, 1, 3, 4)
    got = over_all(pieces.reshape(256, 4, HD)).reshape(8, STEPS, 4, 4, HD)
    attended = got.transpose(1, 3, 0, 2, 4).reshape(STEPS, 4, D)
    pieces, marks = last_update(width, place, attended, updated, first_gap)
    totals = jnp.sum(over_all(marks), axis=0)[:, 0]
    residuals = jnp.sqrt(totals / (STEPS * TOKENS * D))
    return (deliver(place, pieces)[None], residuals)


def solution(mesh):
    fine = Mesh(mesh.devices.reshape(4, 2, 8, 4), ALL)
    placed = (P(), P(STEP, SEQ, None), P(None, None, SEQ))
    return jax.shard_map(
        local, mesh=fine, in_specs=placed, out_specs=(P(STEP, SEQ, None), P()), check_vma=False
    )
```
